256 devices in a mesh: ctx: 64 (over y, z, core), head: 4 (over x).
Axes of the slice: x: 4, y: 4, z: 8, core: 2. Of those that a mesh axis runs over, the one named last changes fastest.
Arguments:
- tokens: bfloat16 [32768, 4096], P('ctx', 'head'), may hold values from -16 to 16
- w_query: bfloat16 [4096, 2048], P(None, 'head'), as said below
- w_key: bfloat16 [4096, 2048], P(None, 'head'), as said below
- w_value: bfloat16 [4096, 2048], P(None, 'head'), as said below
- gate_logit: float32 [16], P('head'), may hold values from -1 to 3
Outputs:
- attended: bfloat16 [32768, 2048], P('ctx', 'head')
The draws below stay inside these ranges and needn't reach their ends.
Inputs may be any that keep to these rules, and one draw needn't show every extreme that they name: `w_query`: entries of order 4096 ** -0.5. `w_key`: entries of order 4096 ** -0.5. `w_value`: entries of order 4096 ** -0.5.
All inputs are finite; a program needn't handle non-finite values.
Results may differ from the reference program's by a relative error of at most 0.0098.
Values may be sent and summed in bfloat16 or wider, within the bound.
A program may use at most 128 MiB of HBM per device.

```python
import math
import jax
import jax.numpy as jnp
from jax import lax

D = 4096
HEADS = 16
HD = 128
TOK_DEV = 512
TOKENS = 32768


def bias_vector(key):
    return jnp.clip(jax.random.normal(jax.random.fold_in(key, 51), (D,), jnp.float32), -3.0, 3.0)


def bias_columns(key):
    return -14.0 / D * bias_vector(key)[:, None] + jnp.zeros((1, HEADS * HD), jnp.float32)


def segment_offsets(key):
    count = TOKENS // TOK_DEV
    common = jax.random.normal(jax.random.fold_in(key, 41), (1, D), jnp.float32)
    own = jax.random.normal(jax.random.fold_in(key, 42), (count, D), jnp.float32)
    shift = 0.5 * jnp.clip(common, -6.0, 6.0) + 0.6 * jnp.clip(own, -6.0, 6.0)
    level = jnp.exp(jax.random.uniform(jax.random.fold_in(key, 43), (count, 1), jnp.float32, minval=math.log(0.5), maxval=math.log(2.8)))
    return (jnp.repeat(shift, TOK_DEV, axis=0), jnp.repeat(level, TOK_DEV, axis=0))


def draw_tokens(key, part):
    samples = jax.random.normal(jax.random.fold_in(key, 21), (TOKENS, D), jnp.float32)
    shift_rows, level_rows = segment_offsets(key)
    offset_row = 0.25 * bias_vector(key)[None, :]
    rows_out = level_rows * (jnp.clip(samples, -6.0, 6.0) + shift_rows) + offset_row
    return jnp.clip(rows_out, -16.0, 16.0).astype(jnp.bfloat16)


def shared_projection(key):
    samples = jax.random.normal(jax.random.fold_in(key, 31), (D, HEADS * HD), jnp.float32)
    return jnp.clip(samples, -6.0, 6.0) / math.sqrt(D)


def fresh_projection(key, number):
    samples = jax.random.normal(jax.random.fold_in(key, number), (D, HEADS * HD), jnp.float32)
    return jnp.clip(samples, -6.0, 6.0) / math.sqrt(D)


def draw_w_query(key, part):
    return (shared_projection(key) + bias_columns(key)).astype(jnp.bfloat16)


def draw_w_key(key, part):
    return (fresh_projection(key, 33) + bias_columns(key)).astype(jnp.bfloat16)


def draw_w_value(key, part):
    base = fresh_projection(key, 33)
    return (0.9 * base + 0.44 * fresh_projection(key, 34)).astype(jnp.bfloat16)


def steps_of(key, shape, shards, low, high):
    level, own = 1.0, jax.random.fold_in(key, 6)
    for dim, blocks in shards:
        steps = jnp.exp(jax.random.uniform(jax.random.fold_in(own, dim), (blocks,), jnp.float32, low / len(shards), high / len(shards)))
        level = level * jnp.repeat(steps, shape[dim] // blocks).reshape([-1 if axis == dim else 1 for axis in range(len(shape))])
    return level


def setup_inputs(seed: int = 0) -> dict:
    keys = jax.random.split(jax.random.key(seed), 6)
    return {
        "tokens": draw_tokens(jax.random.fold_in(keys[5], 71), 0),
        "w_query": draw_w_query(jax.random.fold_in(keys[5], 71), 0),
        "w_key": draw_w_key(jax.random.fold_in(keys[5], 71), 0),
        "w_value": draw_w_value(jax.random.fold_in(keys[5], 71), 0),
        "gate_logit": jnp.clip(-1.0 + 4.0 * jax.random.uniform(keys[4], (HEADS,), jnp.float32) ** steps_of(keys[4], (HEADS,), ((0, 4),), -0.2, 0.2), -1.0, 3.0),
    }


def feature_map(inputs_arr):
    return jax.nn.elu(inputs_arr) + 1.0

def reference(tokens, w_query, w_key, w_value, gate_logit):
    queries = jnp.dot(tokens, w_query, preferred_element_type=jnp.float32).astype(jnp.bfloat16)
    key_rows = jnp.dot(tokens, w_key, preferred_element_type=jnp.float32).astype(jnp.bfloat16)
    values = jnp.dot(tokens, w_value, preferred_element_type=jnp.float32).astype(jnp.bfloat16)
    segments = TOKENS // TOK_DEV
    queries = queries.reshape(segments, TOK_DEV, HEADS, HD)
    key_rows = key_rows.reshape(segments, TOK_DEV, HEADS, HD)
    values = values.reshape(segments, TOK_DEV, HEADS, HD)
    mapped_keys = feature_map(key_rows.astype(jnp.float32)).astype(jnp.bfloat16)

    def segment_update(inputs_pair):
        mapped, seg_values = inputs_pair
        mapped = mapped.astype(jnp.float32)
        update = jnp.einsum('thd,the->hde', mapped, seg_values.astype(jnp.float32))
        return (update, lax.optimization_barrier(jnp.sum(mapped, axis=0)))
    updates, norm_updates = lax.map(segment_update, (mapped_keys, values))
    memory = jnp.concatenate([jnp.zeros_like(updates[:1]), jnp.cumsum(updates, axis=0)[:-1]], axis=0)
    normalizer = jnp.concatenate([jnp.zeros_like(norm_updates[:1]), jnp.cumsum(norm_updates, axis=0)[:-1]], axis=0)
    gate_share = jax.nn.sigmoid(gate_logit.astype(jnp.float32))

    def segment_output(segment_items):
        seg_q, seg_k, seg_v, seg_memory, seg_norm = segment_items
        mapped_query = feature_map(seg_q.astype(jnp.float32))
        numerator = jnp.einsum('thd,hde->the', mapped_query, seg_memory, precision=lax.Precision.HIGHEST)
        denominator = jnp.einsum('thd,hd->th', mapped_query, seg_norm, precision=lax.Precision.HIGHEST)
        retrieved = numerator / jnp.maximum(denominator, 1.0)[:, :, None]
        scores = jnp.einsum('thd,uhd->htu', seg_q.astype(jnp.float32), seg_k.astype(jnp.float32)) / math.sqrt(HD)
        causal = jnp.arange(TOK_DEV)[:, None] >= jnp.arange(TOK_DEV)[None, :]
        scores = jnp.where(causal[None], scores, -jnp.inf)
        row_max = lax.optimization_barrier(jnp.max(scores, axis=-1, keepdims=True))
        weights = jnp.exp(scores - row_max)
        probs = (weights / lax.optimization_barrier(jnp.sum(weights, axis=-1, keepdims=True))).astype(jnp.bfloat16)
        local_part = jnp.einsum('htu,uhd->thd', probs.astype(jnp.float32), seg_v.astype(jnp.float32))
        mixed = gate_share[None, :, None] * retrieved + (1.0 - gate_share)[None, :, None] * local_part
        return mixed.astype(jnp.bfloat16)
    outputs = lax.map(segment_output, (queries, key_rows, values, memory, normalizer))
    return outputs.reshape(TOKENS, HEADS * HD)
```

```python
import functools
import math

import jax
import jax.numpy as jnp
from jax import lax
from jax.experimental import pallas as pl
from jax.experimental.pallas import tpu as pltpu
from jax.sharding import PartitionSpec as P

MESH = pl.DeviceIdType.MESH
F32, BF16 = jnp.float32, jnp.bfloat16
HD = 128
TOK = 512
WIDTH = 512
DEPTH = 1024
HEADS = 4
ROWDEV = 16
YS = 4
SLICE = 32
MSG = 48
CHUNKS = ((0, 128), (128, 128), (256, 128), (384, 128))
AHEAD = 2
FAR_FIRST = (8, 7, 9, 6, 10, 5, 11, 4, 12, 3, 13, 2, 14, 1, 15)


def phi(u):
    return jnp.where(u > 0, u + 1.0, jnp.exp(jnp.minimum(u, 0.0)))


def dot(a, b):
    return jnp.dot(a, b, preferred_element_type=F32)


def kernel(
    tok_hbm, wq_hbm, wk_hbm, wv_hbm, gate_ref, out_ref,
    tok, weights, qkv, acc, update, norm, mapped_q, local, scale,
    send1, got1, send2, got2, prefix, send3, memory,
    load_sem, x_send, x_recv, s_send, s_recv,
):
    me = lax.axis_index("ctx")
    x = lax.axis_index("head")
    col, row = lax.rem(me, ROWDEV), me // ROWDEV
    right, left = {"head": lax.rem(x + 1, 4)}, {"head": lax.rem(x + 3, 4)}
    sides = (right, left)

    def in_row(d):
        return {"ctx": row * ROWDEV + lax.rem(col + d, ROWDEV)}

    def in_column(d):
        return {"ctx": lax.rem(row + d, YS) * ROWDEV + col}

    loads = [pltpu.make_async_copy(tok_hbm, tok.at[0], load_sem.at[0])]
    for p, w in enumerate((wq_hbm, wk_hbm, wv_hbm)):
        loads.append(pltpu.make_async_copy(w, weights.at[p], load_sem.at[1 + p]))
    for load in loads:
        load.start()

    barrier = pltpu.get_barrier_semaphore()
    partners = [in_row(d) for d in FAR_FIRST] + [in_column(d) for d in (2, 1, 3)] + [right, left]
    for target in partners:
        pl.semaphore_signal(barrier, inc=1, device_id=target, device_id_type=MESH)
    pl.semaphore_wait(barrier, len(partners))

    def own(c, j):
        rows = pl.ds(*CHUNKS[c])
        return pltpu.make_async_remote_copy(
            src_ref=tok_hbm.at[rows], dst_ref=tok.at[1 + j, rows],
            send_sem=x_send.at[j, c], recv_sem=x_recv.at[j, c],
            device_id=sides[j], device_id_type=MESH,
        )

    def forward(c, j):
        first, count = CHUNKS[c]
        rows = pl.ds(first + j * (count // 2), count // 2)
        return pltpu.make_async_remote_copy(
            src_ref=tok.at[1 + j, rows], dst_ref=tok.at[3, rows],
            send_sem=x_send.at[2 + j, c], recv_sem=x_recv.at[2 + j, c],
            device_id=sides[j], device_id_type=MESH,
        )

    sources = (x, lax.rem(x + 3, 4), lax.rem(x + 1, 4), lax.rem(x + 2, 4))

    def partial_sum(p, c, which):
        rows = pl.ds(*CHUNKS[c])
        return sum(dot(tok[s, rows, :], weights[p, sources[s]]) for s in which)

    def keep(p, c, total):
        total = total.astype(BF16)
        for h in range(HEADS):
            qkv[p, h, pl.ds(*CHUNKS[c]), :] = total[:, h * HD : (h + 1) * HD]

    def add_update(c):
        rows = pl.ds(*CHUNKS[c])

        def head(h, carry):
            mapped = phi(qkv[1, h, rows, :].astype(F32)).astype(BF16)
            new = lax.dot_general(
                mapped, qkv[2, h, rows, :], (((0,), (0,)), ((), ())), preferred_element_type=F32
            )
            new_norm = dot(jnp.ones((16, CHUNKS[c][1]), BF16), mapped)
            if c == 0:
                update[h] = new
                norm[h] = new_norm
            else:
                update[h] += new
                norm[h] += new_norm
            return carry

        lax.fori_loop(0, HEADS, head, 0)

    last = len(CHUNKS) - 1
    for c in range(AHEAD):
        for j in range(2):
            own(c, j).start()
    for load in loads:
        load.wait()
    for c in range(last + 1):
        for j in range(2):
            own(c, j).wait_recv()
            forward(c, j).start()
        if c + AHEAD <= last:
            for j in range(2):
                own(c + AHEAD, j).start()
        if c > 0:
            for j in range(2):
                forward(c - 1, j).wait_recv()

            def project(p, carry, c=c):
                keep(p, c - 1, partial_sum(p, c - 1, (0, 1, 2, 3)))
                return carry

            lax.fori_loop(0, 3, project, 0)
            add_update(c - 1)

    def begin(p, carry):
        acc[p] = partial_sum(p, last, (0, 1, 2))
        return carry

    lax.fori_loop(0, 3, begin, 0)
    for j in range(2):
        forward(last, j).wait_recv()

    def finish(p, carry):
        keep(p, last, acc[p] + partial_sum(p, last, (3,)))
        return carry

    lax.fori_loop(1, 3, finish, 0)
    add_update(last)

    tile_row = lax.broadcasted_iota(jnp.int32, (16, HD), 0)
    tile = jnp.zeros((16, HD), F32)
    for h in range(HEADS):
        high = norm[h].astype(BF16).astype(F32)
        tile = jnp.where(tile_row == h, high, tile)
        tile = jnp.where(tile_row == HEADS + h, norm[h] - high, tile)
    tile = tile.astype(BF16)
    for h in range(HEADS):
        send1[4 * h : 4 * h + 4, 0:SLICE, :] = update[h].reshape(4, SLICE, HD).astype(BF16)
    for d in range(ROWDEV):
        send1[d, SLICE:MSG, :] = tile

    def exchange(step, src, dst):
        for d in FAR_FIRST:
            pltpu.make_async_remote_copy(
                src_ref=src.at[lax.rem(col + d, ROWDEV)], dst_ref=dst.at[col],
                send_sem=s_send.at[step], recv_sem=s_recv.at[step],
                device_id=in_row(d), device_id_type=MESH,
            ).start()
        dst[col] = src[col]

    def all_of(step, src, dst, count):
        return pltpu.make_async_remote_copy(
            src_ref=src.at[pl.ds(0, count)], dst_ref=dst.at[pl.ds(0, count)],
            send_sem=s_send.at[step], recv_sem=s_recv.at[step],
            device_id=right, device_id_type=MESH,
        )

    def attend(h, carry):
        q, k, v = qkv.at[0, h], qkv.at[1, h], qkv.at[2, h]
        mapped_q[h] = phi(q[...].astype(F32)).astype(BF16)
        share = jax.nn.sigmoid(jnp.full((8, HD), gate_ref[h], F32))[0:1, :]
        for i in range(4):
            mine, seen = pl.ds(i * 128, 128), (i + 1) * 128
            scores = lax.dot_general(
                q[mine, :], k[0:seen, :], (((1,), (1,)), ((), ())), preferred_element_type=F32
            ) * (1.0 / math.sqrt(HD))
            at = lax.broadcasted_iota(jnp.int32, (128, seen), 0) + i * 128
            of = lax.broadcasted_iota(jnp.int32, (128, seen), 1)
            scores = jnp.where(of <= at, scores, -jnp.inf)
            w = jnp.exp(scores - jnp.max(scores, axis=-1, keepdims=True))
            probs = (w / jnp.sum(w, axis=-1, keepdims=True)).astype(BF16)
            local[h, mine, :] = (1.0 - share) * dot(probs, v[0:seen, :])
        return carry

    exchange(0, send1, got1)
    lax.fori_loop(0, 1, finish, 0)
    lax.fori_loop(0, 2, attend, 0)
    all_of(0, send1, got1, ROWDEV - 1).wait_recv()

    running = jnp.zeros((MSG, HD), F32)
    for s in range(ROWDEV):
        prefix[s] = running
        running = running + got1[s].astype(F32)
    send2[...] = running.astype(BF16)
    for d in (2, 1, 3):
        pltpu.make_async_remote_copy(
            src_ref=send2, dst_ref=got2.at[row], send_sem=s_send.at[1], recv_sem=s_recv.at[1],
            device_id=in_column(d), device_id_type=MESH,
        ).start()
    got2[row] = send2[...]
    lax.fori_loop(2, 3, attend, 0)
    all_of(1, got2, got2, YS - 1).wait_recv()

    offset = jnp.zeros((MSG, HD), F32)
    for r in range(YS):
        offset = offset + jnp.where(r < row, got2[r].astype(F32), 0.0)
    for s in range(ROWDEV):
        send3[s] = (prefix[s, 0:SLICE, :] + offset[0:SLICE, :]).astype(BF16)
    exchange(2, send3, memory)
    lax.fori_loop(3, 4, attend, 0)

    total_norm = prefix[col, SLICE:MSG, :] + offset[SLICE:MSG, :]
    for h in range(HEADS):
        normalizer = total_norm[h : h + 1, :] + total_norm[HEADS + h : HEADS + h + 1, :]
        share = jax.nn.sigmoid(jnp.full((8, HD), gate_ref[h], F32))[0:1, :]
        below = jnp.sum(mapped_q[h].astype(F32) * normalizer, axis=-1, keepdims=True)
        scale[h] = share / jnp.maximum(below, 1.0)
    all_of(2, send3, memory, ROWDEV - 1).wait_recv()

    for h in range(HEADS):
        held = memory[4 * h : 4 * h + 4].reshape(HD, HD)
        out_ref[:, h * HD : (h + 1) * HD] = (
            scale[h] * dot(mapped_q[h], held) + local[h]
        ).astype(BF16)

    for c in range(last + 1):
        for j in range(2):
            own(c, j).wait_send()
            forward(c, j).wait_send()
    all_of(0, send1, got1, ROWDEV - 1).wait_send()
    all_of(1, got2, got2, YS - 1).wait_send()
    all_of(2, send3, memory, ROWDEV - 1).wait_send()


def per_device(tokens, w_query, w_key, w_value, gate_logit):
    weights = tuple(w.reshape(4, DEPTH, WIDTH) for w in (w_query, w_key, w_value))
    anywhere = pl.BlockSpec(memory_space=pl.ANY)
    steps = len(CHUNKS)
    return pl.pallas_call(
        kernel,
        out_shape=jax.ShapeDtypeStruct((TOK, WIDTH), BF16),
        in_specs=[anywhere] * 4 + [pl.BlockSpec(memory_space=pltpu.SMEM)],
        out_specs=pl.BlockSpec(memory_space=pltpu.VMEM),
        scratch_shapes=[
            pltpu.VMEM((4, TOK, DEPTH), BF16),
            pltpu.VMEM((3, 4, DEPTH, WIDTH), BF16),
            pltpu.VMEM((3, HEADS, TOK, HD), BF16),
            pltpu.VMEM((3, CHUNKS[-1][1], WIDTH), F32),
            pltpu.VMEM((HEADS, HD, HD), F32),
            pltpu.VMEM((HEADS, 16, HD), F32),
            pltpu.VMEM((HEADS, TOK, HD), BF16),
            pltpu.VMEM((HEADS, TOK, HD), F32),
            pltpu.VMEM((HEADS, TOK, HD), F32),
            pltpu.VMEM((ROWDEV, MSG, HD), BF16),
            pltpu.VMEM((ROWDEV, MSG, HD), BF16),
            pltpu.VMEM((MSG, HD), BF16),
            pltpu.VMEM((YS, MSG, HD), BF16),
            pltpu.VMEM((ROWDEV, MSG, HD), F32),
            pltpu.VMEM((ROWDEV, SLICE, HD), BF16),
            pltpu.VMEM((ROWDEV, SLICE, HD), BF16),
            pltpu.SemaphoreType.DMA((4,)),
            pltpu.SemaphoreType.DMA((4, steps)),
            pltpu.SemaphoreType.DMA((4, steps)),
            pltpu.SemaphoreType.DMA((3,)),
            pltpu.SemaphoreType.DMA((3,)),
        ],
        compiler_params=pltpu.CompilerParams(
            collective_id=0, has_side_effects=True, vmem_limit_bytes=48 << 20
        ),
        cost_estimate=pl.CostEstimate(
            flops=7_400_000_000, bytes_accessed=15_000_000, transcendentals=2_000_000
        ),
    )(tokens, *weights, gate_logit)


def solution(mesh):
    return jax.shard_map(
        per_device,
        mesh=mesh,
        in_specs=(P("ctx", "head"), P(None, "head"), P(None, "head"), P(None, "head"), P("head")),
        out_specs=P("ctx", "head"),
        check_vma=False,
    )
```

```python
import functools
import math

import jax
import jax.numpy as jnp
from jax import lax
from jax.experimental import pallas as pl
from jax.experimental.pallas import tpu as pltpu
from jax.sharding import PartitionSpec as P

MESH = pl.DeviceIdType.MESH
F32, BF16 = jnp.float32, jnp.bfloat16
HD = 128
TOK = 512
WIDTH = 512
DEPTH = 1024
HEADS = 4
ROWDEV = 16
YS = 4
SLICE = 32
MSG = 48
SIZES = (128, 128, 128, 128)
CHUNKS = tuple((sum(SIZES[:i]), n) for i, n in enumerate(SIZES))
AHEAD = 2
DIRECT = 0
FAR_FIRST = (8, 7, 9, 6, 10, 5, 11, 4, 12, 3, 13, 2, 14, 1, 15)


def phi(u):
    return jnp.where(u > 0, u + 1.0, jnp.exp(jnp.minimum(u, 0.0)))


def dot(a, b):
    return jnp.dot(a, b, preferred_element_type=F32)


def kernel(
    tok_hbm, wq_hbm, wk_hbm, wv_hbm, gate_hbm, out_ref,
    tok, weights, gate_ref, qkv, acc, update, norm, mapped_q, local, scale,
    send1, got1, send2, got2, prefix, send3, memory,
    load_sem, x_send, x_recv, s_send, s_recv, met,
):
    me = lax.axis_index("ctx")
    x = lax.axis_index("head")
    col, row = lax.rem(me, ROWDEV), me // ROWDEV
    right, left = {"head": lax.rem(x + 1, 4)}, {"head": lax.rem(x + 3, 4)}
    sides = (right, left)

    def in_row(d):
        return {"ctx": row * ROWDEV + lax.rem(col + d, ROWDEV)}

    def in_column(d):
        return {"ctx": lax.rem(row + d, YS) * ROWDEV + col}

    loads = [
        pltpu.make_async_copy(tok_hbm, tok.at[0], load_sem.at[0]),
        pltpu.make_async_copy(gate_hbm, gate_ref, load_sem.at[4]),
    ]
    for p, w in enumerate((wq_hbm, wk_hbm, wv_hbm)):
        loads.append(pltpu.make_async_copy(w, weights.at[p], load_sem.at[1 + p]))
    for load in loads:
        load.start()

    barrier = pltpu.get_barrier_semaphore()
    near = [in_row(2), in_row(14), in_column(1), in_column(3)]
    other = {"ctx": me + 1 - 2 * lax.rem(me, 2)}
    for target in near + [other, right, left]:
        pl.semaphore_signal(barrier, inc=1, device_id=target, device_id_type=MESH)
    pl.semaphore_wait(barrier, len(near) + 3)

    def meet(step):
        for target in (near, [in_row(4), in_row(12)], [in_row(8)])[step]:
            pl.semaphore_signal(met.at[step], inc=1, device_id=target, device_id_type=MESH)

    def met_all(step):
        pl.semaphore_wait(met.at[step], (4, 2, 1)[step])

    def own(c, j):
        rows = pl.ds(*CHUNKS[c])
        return pltpu.make_async_remote_copy(
            src_ref=tok_hbm.at[rows], dst_ref=tok.at[1 + j, rows],
            send_sem=x_send.at[j, c], recv_sem=x_recv.at[j, c],
            device_id=sides[j], device_id_type=MESH,
        )

    last = len(CHUNKS) - 1

    def forward(c, j):
        first, count = CHUNKS[c]
        rows = pl.ds(first + j * (count // 2), count // 2)
        return pltpu.make_async_remote_copy(
            src_ref=tok.at[1 + j, rows], dst_ref=tok.at[3, rows],
            send_sem=x_send.at[2 + j, c], recv_sem=x_recv.at[2 + j, c],
            device_id=sides[j], device_id_type=MESH,
        )

    def straight(c):
        rows = pl.ds(*CHUNKS[c])
        return pltpu.make_async_remote_copy(
            src_ref=tok_hbm.at[rows], dst_ref=tok.at[3, rows],
            send_sem=x_send.at[2, c], recv_sem=x_recv.at[2, c],
            device_id={"head": lax.rem(x + 2, 4)}, device_id_type=MESH,
        )

    def to_opposite(c):
        return [straight(c)] if c > last - DIRECT else [forward(c, 0), forward(c, 1)]

    sources = (x, lax.rem(x + 3, 4), lax.rem(x + 1, 4), lax.rem(x + 2, 4))

    def partial_sum(p, c, which):
        rows = pl.ds(*CHUNKS[c])
        return sum(dot(tok[s, rows, :], weights[p, sources[s]]) for s in which)

    def keep(p, c, total):
        total = total.astype(BF16)
        for h in range(HEADS):
            qkv[p, h, pl.ds(*CHUNKS[c]), :] = total[:, h * HD : (h + 1) * HD]

    def add_update(c):
        rows = pl.ds(*CHUNKS[c])

        def head(h, carry):
            mapped = phi(qkv[1, h, rows, :].astype(F32)).astype(BF16)
            new = lax.dot_general(
                mapped, qkv[2, h, rows, :], (((0,), (0,)), ((), ())), preferred_element_type=F32
            )
            new_norm = dot(jnp.ones((16, CHUNKS[c][1]), BF16), mapped)
            if c == 0:
                update[h] = new
                norm[h] = new_norm
            else:
                update[h] += new
                norm[h] += new_norm
            return carry

        lax.fori_loop(0, HEADS, head, 0, unroll=True)

    def start_own(c):
        for j in range(2):
            own(c, j).start()
        if c > last - DIRECT:
            straight(c).start()

    meet(0)
    for c in range(AHEAD):
        start_own(c)
    for load in loads:
        load.wait()
    for c in range(last + 1):
        for j in range(2):
            own(c, j).wait_recv()
            if c <= last - DIRECT:
                forward(c, j).start()
        if c + AHEAD <= last:
            start_own(c + AHEAD)
        if c < 3:
            met_all(c)
            if c < 2:
                meet(c + 1)
        if c > 0:
            for copy in to_opposite(c - 1):
                copy.wait_recv()

            def project(p, carry, c=c):
                keep(p, c - 1, partial_sum(p, c - 1, (0, 1, 2, 3)))
                return carry

            lax.fori_loop(0, 3, project, 0)
            add_update(c - 1)

    for p in (1, 2):
        acc[p - 1] = partial_sum(p, last, (0, 1, 2))
    for copy in to_opposite(last):
        copy.wait_recv()
    for p in (1, 2):
        keep(p, last, acc[p - 1] + partial_sum(p, last, (3,)))
    add_update(last)

    tile_row = lax.broadcasted_iota(jnp.int32, (16, HD), 0)
    tile = jnp.zeros((16, HD), F32)
    for h in range(HEADS):
        high = norm[h].astype(BF16).astype(F32)
        tile = jnp.where(tile_row == h, high, tile)
        tile = jnp.where(tile_row == HEADS + h, norm[h] - high, tile)
    tile = tile.astype(BF16)
    for h in range(HEADS):
        send1[4 * h : 4 * h + 4, 0:SLICE, :] = update[h].reshape(4, SLICE, HD).astype(BF16)
    for d in range(ROWDEV):
        send1[d, SLICE:MSG, :] = tile

    def exchange(step, src, dst):
        for d in FAR_FIRST:
            pltpu.make_async_remote_copy(
                src_ref=src.at[lax.rem(col + d, ROWDEV)], dst_ref=dst.at[col],
                send_sem=s_send.at[step], recv_sem=s_recv.at[step],
                device_id=in_row(d), device_id_type=MESH,
            ).start()
        dst[col] = src[col]

    def all_of(step, src, dst, count):
        return pltpu.make_async_remote_copy(
            src_ref=src.at[pl.ds(0, count)], dst_ref=dst.at[pl.ds(0, count)],
            send_sem=s_send.at[step], recv_sem=s_recv.at[step],
            device_id=right, device_id_type=MESH,
        )

    def attend(h, carry):
        q, k, v = qkv.at[0, h], qkv.at[1, h], qkv.at[2, h]
        mapped_q[h] = phi(q[...].astype(F32)).astype(BF16)
        share = jax.nn.sigmoid(jnp.full((8, HD), gate_ref[h], F32))[0:1, :]
        for i in range(4):
            mine, seen = pl.ds(i * 128, 128), (i + 1) * 128
            scores = lax.dot_general(
                q[mine, :], k[0:seen, :], (((1,), (1,)), ((), ())), preferred_element_type=F32
            ) * (1.0 / math.sqrt(HD))
            at = lax.broadcasted_iota(jnp.int32, (128, seen), 0) + i * 128
            of = lax.broadcasted_iota(jnp.int32, (128, seen), 1)
            scores = jnp.where(of <= at, scores, -jnp.inf)
            w = jnp.exp(scores - jnp.max(scores, axis=-1, keepdims=True))
            probs = (w / jnp.sum(w, axis=-1, keepdims=True)).astype(BF16)
            local[h, mine, :] = (1.0 - share) * dot(probs, v[0:seen, :])
        return carry

    exchange(0, send1, got1)
    keep(0, last, partial_sum(0, last, (0, 1, 2, 3)))
    lax.fori_loop(0, 2, attend, 0)
    all_of(0, send1, got1, ROWDEV - 1).wait_recv()

    total = got1[0].astype(F32)
    for s in range(1, ROWDEV):
        total = total + got1[s].astype(F32)
    send2[...] = total.astype(BF16)
    for d in (2, 1, 3):
        pltpu.make_async_remote_copy(
            src_ref=send2, dst_ref=got2.at[row], send_sem=s_send.at[1], recv_sem=s_recv.at[1],
            device_id=in_column(d), device_id_type=MESH,
        ).start()
    got2[row] = send2[...]
    running = jnp.zeros((MSG, HD), F32)
    for s in range(ROWDEV):
        prefix[s] = running
        running = running + got1[s].astype(F32)
    lax.fori_loop(2, 3, attend, 0)
    all_of(1, got2, got2, YS - 1).wait_recv()

    offset = jnp.zeros((MSG, HD), F32)
    for r in range(YS):
        offset = offset + jnp.where(r < row, got2[r].astype(F32), 0.0)
    for s in range(ROWDEV):
        send3[s] = (prefix[s, 0:SLICE, :] + offset[0:SLICE, :]).astype(BF16)
    exchange(2, send3, memory)
    lax.fori_loop(3, 4, attend, 0)

    total_norm = prefix[col, SLICE:MSG, :] + offset[SLICE:MSG, :]
    for h in range(HEADS):
        normalizer = total_norm[h : h + 1, :] + total_norm[HEADS + h : HEADS + h + 1, :]
        share = jax.nn.sigmoid(jnp.full((8, HD), gate_ref[h], F32))[0:1, :]
        below = jnp.sum(mapped_q[h].astype(F32) * normalizer, axis=-1, keepdims=True)
        scale[h] = share / jnp.maximum(below, 1.0)
    all_of(2, send3, memory, ROWDEV - 1).wait_recv()

    for h in range(HEADS):
        held = memory[4 * h : 4 * h + 4].reshape(HD, HD)
        out_ref[:, h * HD : (h + 1) * HD] = (
            scale[h] * dot(mapped_q[h], held) + local[h]
        ).astype(BF16)

    for c in range(last + 1):
        for j in range(2):
            own(c, j).wait_send()
        for copy in to_opposite(c):
            copy.wait_send()
    all_of(0, send1, got1, ROWDEV - 1).wait_send()
    all_of(1, got2, got2, YS - 1).wait_send()
    all_of(2, send3, memory, ROWDEV - 1).wait_send()


def per_device(tokens, w_query, w_key, w_value, gate_logit):
    weights = tuple(w.reshape(4, DEPTH, WIDTH) for w in (w_query, w_key, w_value))
    anywhere = pl.BlockSpec(memory_space=pl.ANY)
    steps = len(CHUNKS)
    return pl.pallas_call(
        kernel,
        out_shape=jax.ShapeDtypeStruct((TOK, WIDTH), BF16),
        in_specs=[anywhere] * 5,
        out_specs=pl.BlockSpec(memory_space=pltpu.VMEM),
        scratch_shapes=[
            pltpu.VMEM((4, TOK, DEPTH), BF16),
            pltpu.VMEM((3, 4, DEPTH, WIDTH), BF16),
            pltpu.SMEM((HEADS,), F32),
            pltpu.VMEM((3, HEADS, TOK, HD), BF16),
            pltpu.VMEM((2, CHUNKS[-1][1], WIDTH), F32),
            pltpu.VMEM((HEADS, HD, HD), F32),
            pltpu.VMEM((HEADS, 16, HD), F32),
            pltpu.VMEM((HEADS, TOK, HD), BF16),
            pltpu.VMEM((HEADS, TOK, HD), F32),
            pltpu.VMEM((HEADS, TOK, HD), F32),
            pltpu.VMEM((ROWDEV, MSG, HD), BF16),
            pltpu.VMEM((ROWDEV, MSG, HD), BF16),
            pltpu.VMEM((MSG, HD), BF16),
            pltpu.VMEM((YS, MSG, HD), BF16),
            pltpu.VMEM((ROWDEV, MSG, HD), F32),
            pltpu.VMEM((ROWDEV, SLICE, HD), BF16),
            pltpu.VMEM((ROWDEV, SLICE, HD), BF16),
            pltpu.SemaphoreType.DMA((5,)),
            pltpu.SemaphoreType.DMA((4, steps)),
            pltpu.SemaphoreType.DMA((4, steps)),
            pltpu.SemaphoreType.DMA((3,)),
            pltpu.SemaphoreType.DMA((3,)),
            pltpu.SemaphoreType.REGULAR((3,)),
        ],
        compiler_params=pltpu.CompilerParams(
            collective_id=0, has_side_effects=True, vmem_limit_bytes=63 << 20
        ),
        cost_estimate=pl.CostEstimate(
            flops=7_400_000_000, bytes_accessed=15_000_000, transcendentals=2_000_000
        ),
    )(tokens, *weights, gate_logit)


def solution(mesh):
    return jax.shard_map(
        per_device,
        mesh=mesh,
        in_specs=(P("ctx", "head"), P(None, "head"), P(None, "head"), P(None, "head"), P("head")),
        out_specs=P("ctx", "head"),
        check_vma=False,
    )
```

```python
import functools
import math

import jax
import jax.numpy as jnp
from jax import lax
from jax.experimental import pallas as pl
from jax.experimental.pallas import tpu as pltpu
from jax.sharding import PartitionSpec as P

MESH = pl.DeviceIdType.MESH
F32, BF16 = jnp.float32, jnp.bfloat16
HD = 128
TOK = 512
WIDTH = 512
DEPTH = 1024
HEADS = 4
ROWDEV = 16
YS = 4
SLICE = 32
TILE = 16
SIZES = (128, 128, 128, 128)
CHUNKS = tuple((sum(SIZES[:i]), n) for i, n in enumerate(SIZES))
AHEAD = 2
DIRECT = 0
FAR_FIRST = (8, 7, 9, 6, 10, 5, 11, 4, 12, 3, 13, 2, 14, 1, 15)
CHIPS_FAR_FIRST = (4, 3, 5, 2, 6, 1, 7)


def phi(u):
    return jnp.where(u > 0, u + 1.0, jnp.exp(jnp.minimum(u, 0.0)))


def dot(a, b):
    return jnp.dot(a, b, preferred_element_type=F32)


def kernel(
    tok_hbm, wq_hbm, wk_hbm, wv_hbm, gate_hbm, out_ref,
    tok, weights, gate_ref, qkv, acc, update, norm, mapped_q, local, scale,
    send1, got1, tile1, tiles1, send2, got2, tile2, tiles2, prefix, send3, memory,
    load_sem, x_send, x_recv, s_send, s_recv, met,
):
    me = lax.axis_index("ctx")
    x = lax.axis_index("head")
    col, row = lax.rem(me, ROWDEV), me // ROWDEV
    chip, core = col // 2, lax.rem(col, 2)
    right, left = {"head": lax.rem(x + 1, 4)}, {"head": lax.rem(x + 3, 4)}
    sides = (right, left)

    def in_row(d):
        return {"ctx": row * ROWDEV + lax.rem(col + d, ROWDEV)}

    def in_column(d):
        return {"ctx": lax.rem(row + d, YS) * ROWDEV + col}

    loads = [
        pltpu.make_async_copy(tok_hbm, tok.at[0], load_sem.at[0]),
        pltpu.make_async_copy(gate_hbm, gate_ref, load_sem.at[4]),
    ]
    for p, w in enumerate((wq_hbm, wk_hbm, wv_hbm)):
        loads.append(pltpu.make_async_copy(w, weights.at[p], load_sem.at[1 + p]))
    for load in loads:
        load.start()

    barrier = pltpu.get_barrier_semaphore()
    near = [in_row(2), in_row(14), in_column(1), in_column(3)]
    other = {"ctx": me + 1 - 2 * lax.rem(me, 2)}
    for target in near + [other, right, left]:
        pl.semaphore_signal(barrier, inc=1, device_id=target, device_id_type=MESH)
    pl.semaphore_wait(barrier, len(near) + 3)

    def meet(step):
        for target in (near, [in_row(4), in_row(12)], [in_row(8)])[step]:
            pl.semaphore_signal(met.at[step], inc=1, device_id=target, device_id_type=MESH)

    def met_all(step):
        pl.semaphore_wait(met.at[step], (4, 2, 1)[step])

    def own(c, j):
        rows = pl.ds(*CHUNKS[c])
        return pltpu.make_async_remote_copy(
            src_ref=tok_hbm.at[rows], dst_ref=tok.at[1 + j, rows],
            send_sem=x_send.at[j, c], recv_sem=x_recv.at[j, c],
            device_id=sides[j], device_id_type=MESH,
        )

    last = len(CHUNKS) - 1

    def forward(c, j):
        first, count = CHUNKS[c]
        rows = pl.ds(first + j * (count // 2), count // 2)
        return pltpu.make_async_remote_copy(
            src_ref=tok.at[1 + j, rows], dst_ref=tok.at[3, rows],
            send_sem=x_send.at[2 + j, c], recv_sem=x_recv.at[2 + j, c],
            device_id=sides[j], device_id_type=MESH,
        )

    def straight(c):
        rows = pl.ds(*CHUNKS[c])
        return pltpu.make_async_remote_copy(
            src_ref=tok_hbm.at[rows], dst_ref=tok.at[3, rows],
            send_sem=x_send.at[2, c], recv_sem=x_recv.at[2, c],
            device_id={"head": lax.rem(x + 2, 4)}, device_id_type=MESH,
        )

    def to_opposite(c):
        return [straight(c)] if c > last - DIRECT else [forward(c, 0), forward(c, 1)]

    sources = (x, lax.rem(x + 3, 4), lax.rem(x + 1, 4), lax.rem(x + 2, 4))

    def partial_sum(p, c, which):
        rows = pl.ds(*CHUNKS[c])
        return sum(dot(tok[s, rows, :], weights[p, sources[s]]) for s in which)

    def keep(p, c, total):
        total = total.astype(BF16)
        for h in range(HEADS):
            qkv[p, h, pl.ds(*CHUNKS[c]), :] = total[:, h * HD : (h + 1) * HD]

    def add_update(c, first=0, count=HEADS):
        rows = pl.ds(*CHUNKS[c])

        def head(h, carry):
            mapped = phi(qkv[1, h, rows, :].astype(F32)).astype(BF16)
            new = lax.dot_general(
                mapped, qkv[2, h, rows, :], (((0,), (0,)), ((), ())), preferred_element_type=F32
            )
            new_norm = dot(jnp.ones((TILE, CHUNKS[c][1]), BF16), mapped)
            if c == 0:
                update[h] = new
                norm[h] = new_norm
            else:
                update[h] += new
                norm[h] += new_norm
            return carry

        lax.fori_loop(first, first + count, head, 0, unroll=True)

    def start_own(c):
        for j in range(2):
            own(c, j).start()
        if c > last - DIRECT:
            straight(c).start()

    meet(0)
    for c in range(AHEAD):
        start_own(c)
    for load in loads:
        load.wait()
    for c in range(last + 1):
        for j in range(2):
            own(c, j).wait_recv()
            if c <= last - DIRECT:
                forward(c, j).start()
        if c + AHEAD <= last:
            start_own(c + AHEAD)
        if c < 3:
            met_all(c)
            if c < 2:
                meet(c + 1)
        if c > 0:
            for copy in to_opposite(c - 1):
                copy.wait_recv()

            def project(p, carry, c=c):
                keep(p, c - 1, partial_sum(p, c - 1, (0, 1, 2, 3)))
                return carry

            lax.fori_loop(0, 3, project, 0)
            add_update(c - 1)

    for p in (1, 2):
        acc[p - 1] = partial_sum(p, last, (0, 1, 2))
    for copy in to_opposite(last):
        copy.wait_recv()
    mine = core * 8 + chip

    def first_step(i, column):
        return pltpu.make_async_remote_copy(
            src_ref=send1.at[i], dst_ref=got1.at[col], send_sem=s_send.at[0], recv_sem=s_recv.at[0],
            device_id={"ctx": row * ROWDEV + column}, device_id_type=MESH,
        )

    rows = pl.ds(*CHUNKS[last])
    for half in range(2):
        columns = pl.ds(half * 256, 256)
        for p in (1, 2):
            total = acc[p - 1, :, columns] + dot(tok[3, rows, :], weights[p, sources[3], :, columns])
            total = total.astype(BF16)
            for h in range(2):
                qkv[p, 2 * half + h, rows, :] = total[:, h * HD : (h + 1) * HD]
        add_update(last, 2 * half, 2)
        for h in (2 * half, 2 * half + 1):
            send1[4 * h : 4 * h + 4] = update[h].reshape(4, SLICE, HD).astype(BF16)
        for d in CHIPS_FAR_FIRST:
            to = lax.rem(chip + d, 8)
            first_step(half * 8 + to, to * 2 + half).start()

        @pl.when(core != half)
        def _(half=half):
            first_step(half * 8 + chip, chip * 2 + half).start()

    got1[col] = send1[mine]

    tile_row = lax.broadcasted_iota(jnp.int32, (TILE, HD), 0)
    tile = jnp.zeros((TILE, HD), F32)
    for h in range(HEADS):
        high = norm[h].astype(BF16).astype(F32)
        tile = jnp.where(tile_row == h, high, tile)
        tile = jnp.where(tile_row == HEADS + h, norm[h] - high, tile)
    tile1[...] = tile.astype(BF16)
    for d in FAR_FIRST:
        pltpu.make_async_remote_copy(
            src_ref=tile1, dst_ref=tiles1.at[col], send_sem=s_send.at[3], recv_sem=s_recv.at[3],
            device_id=in_row(d), device_id_type=MESH,
        ).start()
    tiles1[col] = tile1[...]

    def all_of(step, src, dst, count):
        return pltpu.make_async_remote_copy(
            src_ref=src.at[pl.ds(0, count)], dst_ref=dst.at[pl.ds(0, count)],
            send_sem=s_send.at[step], recv_sem=s_recv.at[step],
            device_id=right, device_id_type=MESH,
        )

    def attend(h, carry):
        q, k, v = qkv.at[0, h], qkv.at[1, h], qkv.at[2, h]
        mapped_q[h] = phi(q[...].astype(F32)).astype(BF16)
        share = jax.nn.sigmoid(jnp.full((8, HD), gate_ref[h], F32))[0:1, :]
        for i in range(4):
            mine, seen = pl.ds(i * 128, 128), (i + 1) * 128
            scores = lax.dot_general(
                q[mine, :], k[0:seen, :], (((1,), (1,)), ((), ())), preferred_element_type=F32
            ) * (1.0 / math.sqrt(HD))
            at = lax.broadcasted_iota(jnp.int32, (128, seen), 0) + i * 128
            of = lax.broadcasted_iota(jnp.int32, (128, seen), 1)
            scores = jnp.where(of <= at, scores, -jnp.inf)
            w = jnp.exp(scores - jnp.max(scores, axis=-1, keepdims=True))
            probs = (w / jnp.sum(w, axis=-1, keepdims=True)).astype(BF16)
            local[h, mine, :] = (1.0 - share) * dot(probs, v[0:seen, :])
        return carry

    keep(0, last, partial_sum(0, last, (0, 1, 2, 3)))
    lax.fori_loop(0, 2, attend, 0)
    all_of(0, got1, got1, ROWDEV - 1).wait_recv()

    def second_step(src, dst, step):
        for d in (2, 1, 3):
            pltpu.make_async_remote_copy(
                src_ref=src, dst_ref=dst.at[row], send_sem=s_send.at[step], recv_sem=s_recv.at[step],
                device_id=in_column(d), device_id_type=MESH,
            ).start()
        dst[row] = src[...]

    total = got1[0].astype(F32)
    for s in range(1, ROWDEV):
        total = total + got1[s].astype(F32)
    send2[...] = total.astype(BF16)
    second_step(send2, got2, 1)
    all_of(3, tiles1, tiles1, ROWDEV - 1).wait_recv()
    total_norm = jnp.zeros((TILE, HD), F32)
    row_norm = jnp.zeros((TILE, HD), F32)
    for s in range(ROWDEV):
        held = tiles1[s].astype(F32)
        total_norm = total_norm + jnp.where(s < col, held, 0.0)
        row_norm = row_norm + held
    tile2[...] = row_norm.astype(BF16)
    second_step(tile2, tiles2, 4)
    running = jnp.zeros((SLICE, HD), F32)
    for s in range(ROWDEV):
        prefix[s] = running
        running = running + got1[s].astype(F32)
    lax.fori_loop(2, 3, attend, 0)
    all_of(1, got2, got2, YS - 1).wait_recv()

    offset = jnp.zeros((SLICE, HD), F32)
    for r in range(YS):
        offset = offset + jnp.where(r < row, got2[r].astype(F32), 0.0)
    for d in FAR_FIRST:
        to = lax.rem(col + d, ROWDEV)
        send3[to] = (prefix[to] + offset).astype(BF16)
        pltpu.make_async_remote_copy(
            src_ref=send3.at[to], dst_ref=memory.at[mine], send_sem=s_send.at[2], recv_sem=s_recv.at[2],
            device_id=in_row(d), device_id_type=MESH,
        ).start()
    memory[mine] = (prefix[col] + offset).astype(BF16)
    lax.fori_loop(3, 4, attend, 0)

    all_of(4, tiles2, tiles2, YS - 1).wait_recv()
    for r in range(YS):
        total_norm = total_norm + jnp.where(r < row, tiles2[r].astype(F32), 0.0)
    for h in range(HEADS):
        normalizer = total_norm[h : h + 1, :] + total_norm[HEADS + h : HEADS + h + 1, :]
        share = jax.nn.sigmoid(jnp.full((8, HD), gate_ref[h], F32))[0:1, :]
        below = jnp.sum(mapped_q[h].astype(F32) * normalizer, axis=-1, keepdims=True)
        scale[h] = share / jnp.maximum(below, 1.0)
    all_of(2, memory, memory, ROWDEV - 1).wait_recv()

    for h in range(HEADS):
        held = memory[4 * h : 4 * h + 4].reshape(HD, HD)
        out_ref[:, h * HD : (h + 1) * HD] = (
            scale[h] * dot(mapped_q[h], held) + local[h]
        ).astype(BF16)

    for c in range(last + 1):
        for j in range(2):
            own(c, j).wait_send()
        for copy in to_opposite(c):
            copy.wait_send()
    all_of(0, got1, got1, ROWDEV - 1).wait_send()
    all_of(1, got2, got2, YS - 1).wait_send()
    all_of(2, memory, memory, ROWDEV - 1).wait_send()
    all_of(3, tiles1, tiles1, ROWDEV - 1).wait_send()
    all_of(4, tiles2, tiles2, YS - 1).wait_send()


def per_device(tokens, w_query, w_key, w_value, gate_logit):
    weights = tuple(w.reshape(4, DEPTH, WIDTH) for w in (w_query, w_key, w_value))
    anywhere = pl.BlockSpec(memory_space=pl.ANY)
    steps = len(CHUNKS)
    return pl.pallas_call(
        kernel,
        out_shape=jax.ShapeDtypeStruct((TOK, WIDTH), BF16),
        in_specs=[anywhere] * 5,
        out_specs=pl.BlockSpec(memory_space=pltpu.VMEM),
        scratch_shapes=[
            pltpu.VMEM((4, TOK, DEPTH), BF16),
            pltpu.VMEM((3, 4, DEPTH, WIDTH), BF16),
            pltpu.SMEM((HEADS,), F32),
            pltpu.VMEM((3, HEADS, TOK, HD), BF16),
            pltpu.VMEM((2, CHUNKS[-1][1], WIDTH), F32),
            pltpu.VMEM((HEADS, HD, HD), F32),
            pltpu.VMEM((HEADS, TILE, HD), F32),
            pltpu.VMEM((HEADS, TOK, HD), BF16),
            pltpu.VMEM((HEADS, TOK, HD), F32),
            pltpu.VMEM((HEADS, TOK, HD), F32),
            pltpu.VMEM((ROWDEV, SLICE, HD), BF16),
            pltpu.VMEM((ROWDEV, SLICE, HD), BF16),
            pltpu.VMEM((TILE, HD), BF16),
            pltpu.VMEM((ROWDEV, TILE, HD), BF16),
            pltpu.VMEM((SLICE, HD), BF16),
            pltpu.VMEM((YS, SLICE, HD), BF16),
            pltpu.VMEM((TILE, HD), BF16),
            pltpu.VMEM((YS, TILE, HD), BF16),
            pltpu.VMEM((ROWDEV, SLICE, HD), F32),
            pltpu.VMEM((ROWDEV, SLICE, HD), BF16),
            pltpu.VMEM((ROWDEV, SLICE, HD), BF16),
            pltpu.SemaphoreType.DMA((5,)),
            pltpu.SemaphoreType.DMA((4, steps)),
            pltpu.SemaphoreType.DMA((4, steps)),
            pltpu.SemaphoreType.DMA((5,)),
            pltpu.SemaphoreType.DMA((5,)),
            pltpu.SemaphoreType.REGULAR((3,)),
        ],
        compiler_params=pltpu.CompilerParams(
            collective_id=0, has_side_effects=True, vmem_limit_bytes=63 << 20
        ),
        cost_estimate=pl.CostEstimate(
            flops=7_400_000_000, bytes_accessed=15_000_000, transcendentals=2_000_000
        ),
    )(tokens, *weights, gate_logit)


def solution(mesh):
    return jax.shard_map(
        per_device,
        mesh=mesh,
        in_specs=(P("ctx", "head"), P(None, "head"), P(None, "head"), P(None, "head"), P("head")),
        out_specs=P("ctx", "head"),
        check_vma=False,
    )
```

```python
import functools
import math

import jax
import jax.numpy as jnp
from jax import lax
from jax.experimental import pallas as pl
from jax.experimental.pallas import tpu as pltpu
from jax.sharding import PartitionSpec as P

MESH = pl.DeviceIdType.MESH
F32, BF16 = jnp.float32, jnp.bfloat16
HD = 128
TOK = 512
WIDTH = 512
DEPTH = 1024
HEADS = 4
ROWDEV = 16
YS = 4
SLICE = 32
TILE = 16
SIZES = (128, 160, 128, 96)
CHUNKS = tuple((sum(SIZES[:i]), n) for i, n in enumerate(SIZES))
AHEAD = 2
DIRECT = 0
FAR_FIRST = (8, 7, 9, 6, 10, 5, 11, 4, 12, 3, 13, 2, 14, 1, 15)
CHIPS_FAR_FIRST = (4, 3, 5, 2, 6, 1, 7)


def phi(u):
    return jnp.where(u > 0, u + 1.0, jnp.exp(jnp.minimum(u, 0.0)))


def dot(a, b):
    return jnp.dot(a, b, preferred_element_type=F32)


def kernel(
    tok_hbm, wq_hbm, wk_hbm, wv_hbm, gate_hbm, out_ref,
    tok, weights, gate_ref, qkv, acc, update, norm, mapped_q, local, scale,
    send1, got1, tile1, tiles1, send2, got2, tile2, tiles2, prefix, send3, memory,
    load_sem, x_send, x_recv, s_send, s_recv, met,
):
    me = lax.axis_index("ctx")
    x = lax.axis_index("head")
    col, row = lax.rem(me, ROWDEV), me // ROWDEV
    chip, core = col // 2, lax.rem(col, 2)
    right, left = {"head": lax.rem(x + 1, 4)}, {"head": lax.rem(x + 3, 4)}
    sides = (right, left)

    def in_row(d):
        return {"ctx": row * ROWDEV + lax.rem(col + d, ROWDEV)}

    def in_column(d):
        return {"ctx": lax.rem(row + d, YS) * ROWDEV + col}

    loads = [
        pltpu.make_async_copy(tok_hbm, tok.at[0], load_sem.at[0]),
        pltpu.make_async_copy(gate_hbm, gate_ref, load_sem.at[4]),
    ]
    for p, w in enumerate((wq_hbm, wk_hbm, wv_hbm)):
        loads.append(pltpu.make_async_copy(w, weights.at[p], load_sem.at[1 + p]))
    for load in loads:
        load.start()

    barrier = pltpu.get_barrier_semaphore()
    near = [in_row(2), in_row(14), in_column(1), in_column(3)]
    other = {"ctx": me + 1 - 2 * lax.rem(me, 2)}
    for target in near + [other, right, left]:
        pl.semaphore_signal(barrier, inc=1, device_id=target, device_id_type=MESH)
    pl.semaphore_wait(barrier, len(near) + 3)

    def meet(step):
        for target in (near, [in_row(4), in_row(12)], [in_row(8)])[step]:
            pl.semaphore_signal(met.at[step], inc=1, device_id=target, device_id_type=MESH)

    def met_all(step):
        pl.semaphore_wait(met.at[step], (4, 2, 1)[step])

    def own(c, j):
        rows = pl.ds(*CHUNKS[c])
        return pltpu.make_async_remote_copy(
            src_ref=tok_hbm.at[rows], dst_ref=tok.at[1 + j, rows],
            send_sem=x_send.at[j, c], recv_sem=x_recv.at[j, c],
            device_id=sides[j], device_id_type=MESH,
        )

    last = len(CHUNKS) - 1

    def forward(c, j):
        first, count = CHUNKS[c]
        rows = pl.ds(first + j * (count // 2), count // 2)
        return pltpu.make_async_remote_copy(
            src_ref=tok.at[1 + j, rows], dst_ref=tok.at[3, rows],
            send_sem=x_send.at[2 + j, c], recv_sem=x_recv.at[2 + j, c],
            device_id=sides[j], device_id_type=MESH,
        )

    def straight(c):
        rows = pl.ds(*CHUNKS[c])
        return pltpu.make_async_remote_copy(
            src_ref=tok_hbm.at[rows], dst_ref=tok.at[3, rows],
            send_sem=x_send.at[2, c], recv_sem=x_recv.at[2, c],
            device_id={"head": lax.rem(x + 2, 4)}, device_id_type=MESH,
        )

    def to_opposite(c):
        return [straight(c)] if c > last - DIRECT else [forward(c, 0), forward(c, 1)]

    sources = (x, lax.rem(x + 3, 4), lax.rem(x + 1, 4), lax.rem(x + 2, 4))

    def partial_sum(p, c, which):
        rows = pl.ds(*CHUNKS[c])
        return sum(dot(tok[s, rows, :], weights[p, sources[s]]) for s in which)

    def keep(p, c, total):
        total = total.astype(BF16)
        for h in range(HEADS):
            qkv[p, h, pl.ds(*CHUNKS[c]), :] = total[:, h * HD : (h + 1) * HD]

    def add_update(c, first=0, count=HEADS):
        rows = pl.ds(*CHUNKS[c])

        def head(h, carry):
            mapped = phi(qkv[1, h, rows, :].astype(F32)).astype(BF16)
            new = lax.dot_general(
                mapped, qkv[2, h, rows, :], (((0,), (0,)), ((), ())), preferred_element_type=F32
            )
            new_norm = dot(jnp.ones((TILE, CHUNKS[c][1]), BF16), mapped)
            if c == 0:
                update[h] = new
                norm[h] = new_norm
            else:
                update[h] += new
                norm[h] += new_norm
            return carry

        lax.fori_loop(first, first + count, head, 0, unroll=True)

    def start_own(c):
        for j in range(2):
            own(c, j).start()
        if c > last - DIRECT:
            straight(c).start()

    meet(0)
    for c in range(AHEAD):
        start_own(c)
    for load in loads:
        load.wait()
    for c in range(last + 1):
        for j in range(2):
            own(c, j).wait_recv()
            if c <= last - DIRECT:
                forward(c, j).start()
        if c + AHEAD <= last:
            start_own(c + AHEAD)
        if c < 3:
            met_all(c)
            if c < 2:
                meet(c + 1)
        def begin(p, carry, c=c):
            acc[p, pl.ds(*CHUNKS[c]), :] = partial_sum(p, c, (0, 1, 2))
            return carry

        lax.fori_loop(0, 3, begin, 0)
        if c > 0:
            for copy in to_opposite(c - 1):
                copy.wait_recv()

            def finish(p, carry, c=c):
                keep(p, c - 1, acc[p, pl.ds(*CHUNKS[c - 1]), :] + partial_sum(p, c - 1, (3,)))
                return carry

            lax.fori_loop(0, 3, finish, 0)
            add_update(c - 1)

    for copy in to_opposite(last):
        copy.wait_recv()
    mine = core * 8 + chip

    def first_step(i, column):
        return pltpu.make_async_remote_copy(
            src_ref=send1.at[i], dst_ref=got1.at[col], send_sem=s_send.at[0], recv_sem=s_recv.at[0],
            device_id={"ctx": row * ROWDEV + column}, device_id_type=MESH,
        )

    rows = pl.ds(*CHUNKS[last])
    for half in range(2):
        columns = pl.ds(half * 256, 256)
        for p in (1, 2):
            total = acc[p, rows, columns] + dot(tok[3, rows, :], weights[p, sources[3], :, columns])
            total = total.astype(BF16)
            for h in range(2):
                qkv[p, 2 * half + h, rows, :] = total[:, h * HD : (h + 1) * HD]
        add_update(last, 2 * half, 2)
        for h in (2 * half, 2 * half + 1):
            send1[4 * h : 4 * h + 4] = update[h].reshape(4, SLICE, HD).astype(BF16)
        for d in CHIPS_FAR_FIRST:
            to = lax.rem(chip + d, 8)
            first_step(half * 8 + to, to * 2 + half).start()

        @pl.when(core != half)
        def _(half=half):
            first_step(half * 8 + chip, chip * 2 + half).start()

    got1[col] = send1[mine]

    tile_row = lax.broadcasted_iota(jnp.int32, (TILE, HD), 0)
    tile = jnp.zeros((TILE, HD), F32)
    for h in range(HEADS):
        high = norm[h].astype(BF16).astype(F32)
        tile = jnp.where(tile_row == h, high, tile)
        tile = jnp.where(tile_row == HEADS + h, norm[h] - high, tile)
    tile1[...] = tile.astype(BF16)
    for d in FAR_FIRST:
        pltpu.make_async_remote_copy(
            src_ref=tile1, dst_ref=tiles1.at[col], send_sem=s_send.at[3], recv_sem=s_recv.at[3],
            device_id=in_row(d), device_id_type=MESH,
        ).start()
    tiles1[col] = tile1[...]

    def all_of(step, src, dst, count):
        return pltpu.make_async_remote_copy(
            src_ref=src.at[pl.ds(0, count)], dst_ref=dst.at[pl.ds(0, count)],
            send_sem=s_send.at[step], recv_sem=s_recv.at[step],
            device_id=right, device_id_type=MESH,
        )

    def attend(h, carry):
        q, k, v = qkv.at[0, h], qkv.at[1, h], qkv.at[2, h]
        mapped_q[h] = phi(q[...].astype(F32)).astype(BF16)
        share = jax.nn.sigmoid(jnp.full((8, HD), gate_ref[h], F32))[0:1, :]
        for i in range(4):
            mine, seen = pl.ds(i * 128, 128), (i + 1) * 128
            scores = lax.dot_general(
                q[mine, :], k[0:seen, :], (((1,), (1,)), ((), ())), preferred_element_type=F32
            ) * (1.0 / math.sqrt(HD))
            at = lax.broadcasted_iota(jnp.int32, (128, seen), 0) + i * 128
            of = lax.broadcasted_iota(jnp.int32, (128, seen), 1)
            scores = jnp.where(of <= at, scores, -jnp.inf)
            w = jnp.exp(scores - jnp.max(scores, axis=-1, keepdims=True))
            probs = (w / jnp.sum(w, axis=-1, keepdims=True)).astype(BF16)
            local[h, mine, :] = (1.0 - share) * dot(probs, v[0:seen, :])
        return carry

    keep(0, last, acc[0, rows, :] + partial_sum(0, last, (3,)))
    lax.fori_loop(0, 2, attend, 0)
    all_of(0, got1, got1, ROWDEV - 1).wait_recv()

    def second_step(src, dst, step):
        for d in (2, 1, 3):
            pltpu.make_async_remote_copy(
                src_ref=src, dst_ref=dst.at[row], send_sem=s_send.at[step], recv_sem=s_recv.at[step],
                device_id=in_column(d), device_id_type=MESH,
            ).start()
        dst[row] = src[...]

    total = got1[0].astype(F32)
    for s in range(1, ROWDEV):
        total = total + got1[s].astype(F32)
    send2[...] = total.astype(BF16)
    second_step(send2, got2, 1)
    all_of(3, tiles1, tiles1, ROWDEV - 1).wait_recv()
    total_norm = jnp.zeros((TILE, HD), F32)
    row_norm = jnp.zeros((TILE, HD), F32)
    for s in range(ROWDEV):
        held = tiles1[s].astype(F32)
        total_norm = total_norm + jnp.where(s < col, held, 0.0)
        row_norm = row_norm + held
    tile2[...] = row_norm.astype(BF16)
    second_step(tile2, tiles2, 4)
    running = jnp.zeros((SLICE, HD), F32)
    for s in range(ROWDEV):
        prefix[s] = running
        running = running + got1[s].astype(F32)
    lax.fori_loop(2, 3, attend, 0)
    all_of(1, got2, got2, YS - 1).wait_recv()

    offset = jnp.zeros((SLICE, HD), F32)
    for r in range(YS):
        offset = offset + jnp.where(r < row, got2[r].astype(F32), 0.0)
    for d in FAR_FIRST:
        to = lax.rem(col + d, ROWDEV)
        send3[to] = (prefix[to] + offset).astype(BF16)
        pltpu.make_async_remote_copy(
            src_ref=send3.at[to], dst_ref=memory.at[mine], send_sem=s_send.at[2], recv_sem=s_recv.at[2],
            device_id=in_row(d), device_id_type=MESH,
        ).start()
    memory[mine] = (prefix[col] + offset).astype(BF16)
    lax.fori_loop(3, 4, attend, 0)

    all_of(4, tiles2, tiles2, YS - 1).wait_recv()
    for r in range(YS):
        total_norm = total_norm + jnp.where(r < row, tiles2[r].astype(F32), 0.0)
    for h in range(HEADS):
        normalizer = total_norm[h : h + 1, :] + total_norm[HEADS + h : HEADS + h + 1, :]
        share = jax.nn.sigmoid(jnp.full((8, HD), gate_ref[h], F32))[0:1, :]
        below = jnp.sum(mapped_q[h].astype(F32) * normalizer, axis=-1, keepdims=True)
        scale[h] = share / jnp.maximum(below, 1.0)
    all_of(2, memory, memory, ROWDEV - 1).wait_recv()

    for h in range(HEADS):
        held = memory[4 * h : 4 * h + 4].reshape(HD, HD)
        out_ref[:, h * HD : (h + 1) * HD] = (
            scale[h] * dot(mapped_q[h], held) + local[h]
        ).astype(BF16)

    for c in range(last + 1):
        for j in range(2):
            own(c, j).wait_send()
        for copy in to_opposite(c):
            copy.wait_send()
    all_of(0, got1, got1, ROWDEV - 1).wait_send()
    all_of(1, got2, got2, YS - 1).wait_send()
    all_of(2, memory, memory, ROWDEV - 1).wait_send()
    all_of(3, tiles1, tiles1, ROWDEV - 1).wait_send()
    all_of(4, tiles2, tiles2, YS - 1).wait_send()


def per_device(tokens, w_query, w_key, w_value, gate_logit):
    weights = tuple(w.reshape(4, DEPTH, WIDTH) for w in (w_query, w_key, w_value))
    anywhere = pl.BlockSpec(memory_space=pl.ANY)
    steps = len(CHUNKS)
    return pl.pallas_call(
        kernel,
        out_shape=jax.ShapeDtypeStruct((TOK, WIDTH), BF16),
        in_specs=[anywhere] * 5,
        out_specs=pl.BlockSpec(memory_space=pltpu.VMEM),
        scratch_shapes=[
            pltpu.VMEM((4, TOK, DEPTH), BF16),
            pltpu.VMEM((3, 4, DEPTH, WIDTH), BF16),
            pltpu.SMEM((HEADS,), F32),
            pltpu.VMEM((3, HEADS, TOK, HD), BF16),
            pltpu.VMEM((3, TOK, WIDTH), F32),
            pltpu.VMEM((HEADS, HD, HD), F32),
            pltpu.VMEM((HEADS, TILE, HD), F32),
            pltpu.VMEM((HEADS, TOK, HD), BF16),
            pltpu.VMEM((HEADS, TOK, HD), F32),
            pltpu.VMEM((HEADS, TOK, HD), F32),
            pltpu.VMEM((ROWDEV, SLICE, HD), BF16),
            pltpu.VMEM((ROWDEV, SLICE, HD), BF16),
            pltpu.VMEM((TILE, HD), BF16),
            pltpu.VMEM((ROWDEV, TILE, HD), BF16),
            pltpu.VMEM((SLICE, HD), BF16),
            pltpu.VMEM((YS, SLICE, HD), BF16),
            pltpu.VMEM((TILE, HD), BF16),
            pltpu.VMEM((YS, TILE, HD), BF16),
            pltpu.VMEM((ROWDEV, SLICE, HD), F32),
            pltpu.VMEM((ROWDEV, SLICE, HD), BF16),
            pltpu.VMEM((ROWDEV, SLICE, HD), BF16),
            pltpu.SemaphoreType.DMA((5,)),
            pltpu.SemaphoreType.DMA((4, steps)),
            pltpu.SemaphoreType.DMA((4, steps)),
            pltpu.SemaphoreType.DMA((5,)),
            pltpu.SemaphoreType.DMA((5,)),
            pltpu.SemaphoreType.REGULAR((3,)),
        ],
        compiler_params=pltpu.CompilerParams(
            collective_id=0, has_side_effects=True, vmem_limit_bytes=63 << 20
        ),
        cost_estimate=pl.CostEstimate(
            flops=7_400_000_000, bytes_accessed=15_000_000, transcendentals=2_000_000
        ),
    )(tokens, *weights, gate_logit)


def solution(mesh):
    return jax.shard_map(
        per_device,
        mesh=mesh,
        in_specs=(P("ctx", "head"), P(None, "head"), P(None, "head"), P(None, "head"), P("head")),
        out_specs=P("ctx", "head"),
        check_vma=False,
    )
```

```python
import functools
import math

import jax
import jax.numpy as jnp
from jax import lax
from jax.experimental import pallas as pl
from jax.experimental.pallas import tpu as pltpu
from jax.sharding import PartitionSpec as P

MESH = pl.DeviceIdType.MESH
F32, BF16 = jnp.float32, jnp.bfloat16
HD = 128
TOK = 512
WIDTH = 512
DEPTH = 1024
HEADS = 4
ROWDEV = 16
YS = 4
SLICE = 32
TILE = 16
SIZES = (128, 160, 128, 96)
CHUNKS = tuple((sum(SIZES[:i]), n) for i, n in enumerate(SIZES))
AHEAD = 2
DIRECT = 0
FAR_FIRST = (8, 7, 9, 6, 10, 5, 11, 4, 12, 3, 13, 2, 14, 1, 15)
TARGETS = (0, 1, 2, 3, 4, 5, 6, 7, 14, 15, 8, 9, 12, 13, 10, 11)
CHIPS_FAR_FIRST = (4, 3, 5, 2, 6, 1, 7)


def phi(u):
    return jnp.where(u > 0, u + 1.0, jnp.exp(jnp.minimum(u, 0.0)))


def dot(a, b):
    return jnp.dot(a, b, preferred_element_type=F32)


def kernel(
    tok_hbm, wq_hbm, wk_hbm, wv_hbm, gate_hbm, out_ref,
    tok, weights, gate_ref, qkv, acc, update, norm, mapped_q, local, scale,
    send1, got1, tile1, tiles1, send2, got2, tile2, tiles2, prefix, offset2, offset_tile, send3, memory,
    load_sem, x_send, x_recv, s_send, s_recv, met,
):
    me = lax.axis_index("ctx")
    x = lax.axis_index("head")
    col, row = lax.rem(me, ROWDEV), me // ROWDEV
    chip, core = col // 2, lax.rem(col, 2)
    right, left = {"head": lax.rem(x + 1, 4)}, {"head": lax.rem(x + 3, 4)}
    sides = (right, left)

    def in_row(d):
        return {"ctx": row * ROWDEV + lax.rem(col + d, ROWDEV)}

    def in_column(d):
        return {"ctx": lax.rem(row + d, YS) * ROWDEV + col}

    loads = [
        pltpu.make_async_copy(tok_hbm, tok.at[0], load_sem.at[0]),
        pltpu.make_async_copy(gate_hbm, gate_ref, load_sem.at[4]),
    ]
    for p, w in enumerate((wq_hbm, wk_hbm, wv_hbm)):
        loads.append(pltpu.make_async_copy(w, weights.at[p], load_sem.at[1 + p]))
    for load in loads:
        load.start()

    barrier = pltpu.get_barrier_semaphore()
    near = [in_row(2), in_row(14), in_column(1), in_column(3)]
    other = {"ctx": me + 1 - 2 * lax.rem(me, 2)}
    for target in near + [other, right, left]:
        pl.semaphore_signal(barrier, inc=1, device_id=target, device_id_type=MESH)
    pl.semaphore_wait(barrier, len(near) + 3)

    def meet(step):
        for target in (near, [in_row(4), in_row(12)], [in_row(8)])[step]:
            pl.semaphore_signal(met.at[step], inc=1, device_id=target, device_id_type=MESH)

    def met_all(step):
        pl.semaphore_wait(met.at[step], (4, 2, 1)[step])

    def own(c, j):
        rows = pl.ds(*CHUNKS[c])
        return pltpu.make_async_remote_copy(
            src_ref=tok_hbm.at[rows], dst_ref=tok.at[1 + j, rows],
            send_sem=x_send.at[j, c], recv_sem=x_recv.at[j, c],
            device_id=sides[j], device_id_type=MESH,
        )

    last = len(CHUNKS) - 1

    def forward(c, j):
        first, count = CHUNKS[c]
        rows = pl.ds(first + j * (count // 2), count // 2)
        return pltpu.make_async_remote_copy(
            src_ref=tok.at[1 + j, rows], dst_ref=tok.at[3, rows],
            send_sem=x_send.at[2 + j, c], recv_sem=x_recv.at[2 + j, c],
            device_id=sides[j], device_id_type=MESH,
        )

    def straight(c):
        rows = pl.ds(*CHUNKS[c])
        return pltpu.make_async_remote_copy(
            src_ref=tok_hbm.at[rows], dst_ref=tok.at[3, rows],
            send_sem=x_send.at[2, c], recv_sem=x_recv.at[2, c],
            device_id={"head": lax.rem(x + 2, 4)}, device_id_type=MESH,
        )

    def to_opposite(c):
        return [straight(c)] if c > last - DIRECT else [forward(c, 0), forward(c, 1)]

    sources = (x, lax.rem(x + 3, 4), lax.rem(x + 1, 4), lax.rem(x + 2, 4))

    def partial_sum(p, c, which):
        rows = pl.ds(*CHUNKS[c])
        return sum(dot(tok[s, rows, :], weights[p, sources[s]]) for s in which)

    def keep(p, c, total):
        total = total.astype(BF16)
        for h in range(HEADS):
            qkv[p, h, pl.ds(*CHUNKS[c]), :] = total[:, h * HD : (h + 1) * HD]

    def add_update(c, first=0, count=HEADS):
        rows = pl.ds(*CHUNKS[c])

        def head(h, carry):
            mapped = phi(qkv[1, h, rows, :].astype(F32)).astype(BF16)
            new = lax.dot_general(
                mapped, qkv[2, h, rows, :], (((0,), (0,)), ((), ())), preferred_element_type=F32
            )
            new_norm = dot(jnp.ones((TILE, CHUNKS[c][1]), BF16), mapped)
            if c == 0:
                update[h] = new
                norm[h] = new_norm
            else:
                update[h] += new
                norm[h] += new_norm
            return carry

        lax.fori_loop(first, first + count, head, 0, unroll=True)

    def start_own(c):
        for j in range(2):
            own(c, j).start()
        if c > last - DIRECT:
            straight(c).start()

    meet(0)
    for c in range(AHEAD):
        start_own(c)
    for load in loads:
        load.wait()
    for c in range(last + 1):
        for j in range(2):
            own(c, j).wait_recv()
            if c <= last - DIRECT:
                forward(c, j).start()
        if c + AHEAD <= last:
            start_own(c + AHEAD)
        if c < 3:
            met_all(c)
            if c < 2:
                meet(c + 1)
        def begin(p, carry, c=c):
            acc[p, pl.ds(*CHUNKS[c]), :] = partial_sum(p, c, (0, 1, 2))
            return carry

        lax.fori_loop(0, 3, begin, 0)
        if c > 0:
            for copy in to_opposite(c - 1):
                copy.wait_recv()

            def finish(p, carry, c=c):
                keep(p, c - 1, acc[p, pl.ds(*CHUNKS[c - 1]), :] + partial_sum(p, c - 1, (3,)))
                return carry

            lax.fori_loop(0, 3, finish, 0)
            add_update(c - 1)

    for copy in to_opposite(last):
        copy.wait_recv()
    mine = core * 8 + chip

    def first_step(i, column):
        return pltpu.make_async_remote_copy(
            src_ref=send1.at[i], dst_ref=got1.at[col], send_sem=s_send.at[0], recv_sem=s_recv.at[0],
            device_id={"ctx": row * ROWDEV + column}, device_id_type=MESH,
        )

    rows = pl.ds(*CHUNKS[last])
    for half in range(2):
        columns = pl.ds(half * 256, 256)
        for p in (1, 2):
            total = acc[p, rows, columns] + dot(tok[3, rows, :], weights[p, sources[3], :, columns])
            total = total.astype(BF16)
            for h in range(2):
                qkv[p, 2 * half + h, rows, :] = total[:, h * HD : (h + 1) * HD]
        add_update(last, 2 * half, 2)
        for h in (2 * half, 2 * half + 1):
            send1[4 * h : 4 * h + 4] = update[h].reshape(4, SLICE, HD).astype(BF16)
        for d in CHIPS_FAR_FIRST:
            to = lax.rem(chip + d, 8)
            first_step(half * 8 + to, to * 2 + half).start()

        @pl.when(core != half)
        def _(half=half):
            first_step(half * 8 + chip, chip * 2 + half).start()

    got1[col] = send1[mine]

    tile_row = lax.broadcasted_iota(jnp.int32, (TILE, HD), 0)
    tile = jnp.zeros((TILE, HD), F32)
    for h in range(HEADS):
        high = norm[h].astype(BF16).astype(F32)
        tile = jnp.where(tile_row == h, high, tile)
        tile = jnp.where(tile_row == HEADS + h, norm[h] - high, tile)
    tile1[...] = tile.astype(BF16)
    for d in FAR_FIRST:
        pltpu.make_async_remote_copy(
            src_ref=tile1, dst_ref=tiles1.at[col], send_sem=s_send.at[3], recv_sem=s_recv.at[3],
            device_id=in_row(d), device_id_type=MESH,
        ).start()
    tiles1[col] = tile1[...]

    def all_of(step, src, dst, count):
        return pltpu.make_async_remote_copy(
            src_ref=src.at[pl.ds(0, count)], dst_ref=dst.at[pl.ds(0, count)],
            send_sem=s_send.at[step], recv_sem=s_recv.at[step],
            device_id=right, device_id_type=MESH,
        )

    def attend(h, carry):
        q, k, v = qkv.at[0, h], qkv.at[1, h], qkv.at[2, h]
        mapped_q[h] = phi(q[...].astype(F32)).astype(BF16)
        share = jax.nn.sigmoid(jnp.full((8, HD), gate_ref[h], F32))[0:1, :]
        for i in range(4):
            mine, seen = pl.ds(i * 128, 128), (i + 1) * 128
            scores = lax.dot_general(
                q[mine, :], k[0:seen, :], (((1,), (1,)), ((), ())), preferred_element_type=F32
            ) * (1.0 / math.sqrt(HD))
            at = lax.broadcasted_iota(jnp.int32, (128, seen), 0) + i * 128
            of = lax.broadcasted_iota(jnp.int32, (128, seen), 1)
            scores = jnp.where(of <= at, scores, -jnp.inf)
            w = jnp.exp(scores - jnp.max(scores, axis=-1, keepdims=True))
            probs = (w / jnp.sum(w, axis=-1, keepdims=True)).astype(BF16)
            local[h, mine, :] = (1.0 - share) * dot(probs, v[0:seen, :])
        return carry

    keep(0, last, acc[0, rows, :] + partial_sum(0, last, (3,)))
    lax.fori_loop(0, 2, attend, 0)
    all_of(0, got1, got1, ROWDEV - 1).wait_recv()

    def second_step(src, dst, step):
        for to in range(1, YS):

            @pl.when(row < to)
            def _(to=to):
                pltpu.make_async_remote_copy(
                    src_ref=src, dst_ref=dst.at[row],
                    send_sem=s_send.at[step], recv_sem=s_recv.at[step],
                    device_id={"ctx": to * ROWDEV + col}, device_id_type=MESH,
                ).start()

    def earlier_rows(dst, step, into):
        into[...] = jnp.zeros_like(into)
        for n in range(1, YS):

            @pl.when(row == n)
            def _(n=n):
                all_of(step, dst, dst, n).wait_recv()
                into[...] = sum(dst[r].astype(F32) for r in range(n))

    total = got1[0].astype(F32)
    for s in range(1, ROWDEV):
        total = total + got1[s].astype(F32)
    send2[...] = total.astype(BF16)
    second_step(send2, got2, 1)
    all_of(3, tiles1, tiles1, ROWDEV - 1).wait_recv()
    total_norm = jnp.zeros((TILE, HD), F32)
    row_norm = jnp.zeros((TILE, HD), F32)
    for s in range(ROWDEV):
        held = tiles1[s].astype(F32)
        total_norm = total_norm + jnp.where(s < col, held, 0.0)
        row_norm = row_norm + held
    tile2[...] = row_norm.astype(BF16)
    second_step(tile2, tiles2, 4)
    running = jnp.zeros((SLICE, HD), F32)
    for s in range(ROWDEV):
        prefix[s] = running
        running = running + got1[s].astype(F32)
    lax.fori_loop(2, 3, attend, 0)

    earlier_rows(got2, 1, offset2)
    offset = offset2[...]
    for to in TARGETS:
        send3[to] = (prefix[to] + offset).astype(BF16)

        @pl.when(col != to)
        def _(to=to):
            pltpu.make_async_remote_copy(
                src_ref=send3.at[to], dst_ref=memory.at[mine],
                send_sem=s_send.at[2], recv_sem=s_recv.at[2],
                device_id={"ctx": row * ROWDEV + to}, device_id_type=MESH,
            ).start()

    memory[mine] = (prefix[col] + offset).astype(BF16)
    lax.fori_loop(3, 4, attend, 0)

    earlier_rows(tiles2, 4, offset_tile)
    total_norm = total_norm + offset_tile[...]
    for h in range(HEADS):
        normalizer = total_norm[h : h + 1, :] + total_norm[HEADS + h : HEADS + h + 1, :]
        share = jax.nn.sigmoid(jnp.full((8, HD), gate_ref[h], F32))[0:1, :]
        below = jnp.sum(mapped_q[h].astype(F32) * normalizer, axis=-1, keepdims=True)
        scale[h] = share / jnp.maximum(below, 1.0)
    all_of(2, memory, memory, ROWDEV - 1).wait_recv()

    for h in range(HEADS):
        held = memory[4 * h : 4 * h + 4].reshape(HD, HD)
        out_ref[:, h * HD : (h + 1) * HD] = (
            scale[h] * dot(mapped_q[h], held) + local[h]
        ).astype(BF16)

    for c in range(last + 1):
        for j in range(2):
            own(c, j).wait_send()
        for copy in to_opposite(c):
            copy.wait_send()
    all_of(0, got1, got1, ROWDEV - 1).wait_send()
    all_of(2, memory, memory, ROWDEV - 1).wait_send()
    all_of(3, tiles1, tiles1, ROWDEV - 1).wait_send()
    for n in range(YS - 1):

        @pl.when(row == n)
        def _(n=n):
            all_of(1, got2, got2, YS - 1 - n).wait_send()
            all_of(4, tiles2, tiles2, YS - 1 - n).wait_send()


def per_device(tokens, w_query, w_key, w_value, gate_logit):
    weights = tuple(w.reshape(4, DEPTH, WIDTH) for w in (w_query, w_key, w_value))
    anywhere = pl.BlockSpec(memory_space=pl.ANY)
    steps = len(CHUNKS)
    return pl.pallas_call(
        kernel,
        out_shape=jax.ShapeDtypeStruct((TOK, WIDTH), BF16),
        in_specs=[anywhere] * 5,
        out_specs=pl.BlockSpec(memory_space=pltpu.VMEM),
        scratch_shapes=[
            pltpu.VMEM((4, TOK, DEPTH), BF16),
            pltpu.VMEM((3, 4, DEPTH, WIDTH), BF16),
            pltpu.SMEM((HEADS,), F32),
            pltpu.VMEM((3, HEADS, TOK, HD), BF16),
            pltpu.VMEM((3, TOK, WIDTH), F32),
            pltpu.VMEM((HEADS, HD, HD), F32),
            pltpu.VMEM((HEADS, TILE, HD), F32),
            pltpu.VMEM((HEADS, TOK, HD), BF16),
            pltpu.VMEM((HEADS, TOK, HD), F32),
            pltpu.VMEM((HEADS, TOK, HD), F32),
            pltpu.VMEM((ROWDEV, SLICE, HD), BF16),
            pltpu.VMEM((ROWDEV, SLICE, HD), BF16),
            pltpu.VMEM((TILE, HD), BF16),
            pltpu.VMEM((ROWDEV, TILE, HD), BF16),
            pltpu.VMEM((SLICE, HD), BF16),
            pltpu.VMEM((YS, SLICE, HD), BF16),
            pltpu.VMEM((TILE, HD), BF16),
            pltpu.VMEM((YS, TILE, HD), BF16),
            pltpu.VMEM((ROWDEV, SLICE, HD), F32),
            pltpu.VMEM((SLICE, HD), F32),
            pltpu.VMEM((TILE, HD), F32),
            pltpu.VMEM((ROWDEV, SLICE, HD), BF16),
            pltpu.VMEM((ROWDEV, SLICE, HD), BF16),
            pltpu.SemaphoreType.DMA((5,)),
            pltpu.SemaphoreType.DMA((4, steps)),
            pltpu.SemaphoreType.DMA((4, steps)),
            pltpu.SemaphoreType.DMA((5,)),
            pltpu.SemaphoreType.DMA((5,)),
            pltpu.SemaphoreType.REGULAR((3,)),
        ],
        compiler_params=pltpu.CompilerParams(
            collective_id=0, has_side_effects=True, vmem_limit_bytes=63 << 20
        ),
        cost_estimate=pl.CostEstimate(
            flops=7_400_000_000, bytes_accessed=15_000_000, transcendentals=2_000_000
        ),
    )(tokens, *weights, gate_logit)


def solution(mesh):
    return jax.shard_map(
        per_device,
        mesh=mesh,
        in_specs=(P("ctx", "head"), P(None, "head"), P(None, "head"), P(None, "head"), P("head")),
        out_specs=P("ctx", "head"),
        check_vma=False,
    )
```

```python
import functools
import math

import jax
import jax.numpy as jnp
from jax import lax
from jax.experimental import pallas as pl
from jax.experimental.pallas import tpu as pltpu
from jax.sharding import PartitionSpec as P

MESH = pl.DeviceIdType.MESH
F32, BF16 = jnp.float32, jnp.bfloat16
HD = 128
TOK = 512
WIDTH = 512
DEPTH = 1024
HEADS = 4
ROWDEV = 16
YS = 4
SLICE = 32
TILE = 16
SIZES = (128, 160, 128, 96)
CHUNKS = tuple((sum(SIZES[:i]), n) for i, n in enumerate(SIZES))
AHEAD = 2
DIRECT = 0
FAR_FIRST = (8, 7, 9, 6, 10, 5, 11, 4, 12, 3, 13, 2, 14, 1, 15)
TARGETS = (0, 1, 2, 3, 4, 5, 6, 7, 14, 15, 8, 9, 12, 13, 10, 11)
CHIPS_FAR_FIRST = (4, 3, 5, 2, 6, 1, 7)


def phi(u):
    return jnp.where(u > 0, u + 1.0, jnp.exp(jnp.minimum(u, 0.0)))


def dot(a, b):
    return jnp.dot(a, b, preferred_element_type=F32)


def kernel(
    tok_hbm, wq_hbm, wk_hbm, wv_hbm, gate_hbm, out_ref,
    tok, weights, gate_ref, qkv, acc, update, norm, mapped_q, local, scale,
    send1, got1, tile1, tiles1, send2, got2, tile2, tiles2, prefix, offset2, offset_tile, send3, memory,
    load_sem, x_send, x_recv, s_send, s_recv, met,
):
    me = lax.axis_index("ctx")
    x = lax.axis_index("head")
    col, row = lax.rem(me, ROWDEV), me // ROWDEV
    chip, core = col // 2, lax.rem(col, 2)
    right, left = {"head": lax.rem(x + 1, 4)}, {"head": lax.rem(x + 3, 4)}
    sides = (right, left)

    def in_row(d):
        return {"ctx": row * ROWDEV + lax.rem(col + d, ROWDEV)}

    def in_column(d):
        return {"ctx": lax.rem(row + d, YS) * ROWDEV + col}

    loads = [
        pltpu.make_async_copy(tok_hbm, tok.at[0], load_sem.at[0]),
        pltpu.make_async_copy(gate_hbm, gate_ref, load_sem.at[4]),
    ]
    for p, w in enumerate((wq_hbm, wk_hbm, wv_hbm)):
        loads.append(pltpu.make_async_copy(w, weights.at[p], load_sem.at[1 + p]))
    for load in loads:
        load.start()

    barrier = pltpu.get_barrier_semaphore()
    near = [in_row(2), in_row(14), in_column(1), in_column(3)]
    other = {"ctx": me + 1 - 2 * lax.rem(me, 2)}
    for target in near + [other, right, left]:
        pl.semaphore_signal(barrier, inc=1, device_id=target, device_id_type=MESH)
    pl.semaphore_wait(barrier, len(near) + 3)

    def meet(step):
        for target in (near, [in_row(4), in_row(12)], [in_row(8)])[step]:
            pl.semaphore_signal(met.at[step], inc=1, device_id=target, device_id_type=MESH)

    def met_all(step):
        pl.semaphore_wait(met.at[step], (4, 2, 1)[step])

    def own(c, j):
        rows = pl.ds(*CHUNKS[c])
        return pltpu.make_async_remote_copy(
            src_ref=tok_hbm.at[rows], dst_ref=tok.at[1 + j, rows],
            send_sem=x_send.at[j, c], recv_sem=x_recv.at[j, c],
            device_id=sides[j], device_id_type=MESH,
        )

    last = len(CHUNKS) - 1

    def forward(c, j):
        first, count = CHUNKS[c]
        rows = pl.ds(first + j * (count // 2), count // 2)
        return pltpu.make_async_remote_copy(
            src_ref=tok.at[1 + j, rows], dst_ref=tok.at[3, rows],
            send_sem=x_send.at[2 + j, c], recv_sem=x_recv.at[2 + j, c],
            device_id=sides[j], device_id_type=MESH,
        )

    def straight(c):
        rows = pl.ds(*CHUNKS[c])
        return pltpu.make_async_remote_copy(
            src_ref=tok_hbm.at[rows], dst_ref=tok.at[3, rows],
            send_sem=x_send.at[2, c], recv_sem=x_recv.at[2, c],
            device_id={"head": lax.rem(x + 2, 4)}, device_id_type=MESH,
        )

    def to_opposite(c):
        return [straight(c)] if c > last - DIRECT else [forward(c, 0), forward(c, 1)]

    sources = (x, lax.rem(x + 3, 4), lax.rem(x + 1, 4), lax.rem(x + 2, 4))

    def partial_sum(p, c, which):
        rows = pl.ds(*CHUNKS[c])
        return sum(dot(tok[s, rows, :], weights[p, sources[s]]) for s in which)

    def keep(p, c, total):
        total = total.astype(BF16)
        for h in range(HEADS):
            qkv[p, h, pl.ds(*CHUNKS[c]), :] = total[:, h * HD : (h + 1) * HD]

    def add_update(c, first=0, count=HEADS):
        rows = pl.ds(*CHUNKS[c])

        def head(h, carry):
            mapped = phi(qkv[1, h, rows, :].astype(F32)).astype(BF16)
            new = lax.dot_general(
                mapped, qkv[2, h, rows, :], (((0,), (0,)), ((), ())), preferred_element_type=F32
            )
            new_norm = dot(jnp.ones((TILE, CHUNKS[c][1]), BF16), mapped)
            if c == 0:
                update[h] = new
                norm[h] = new_norm
            else:
                update[h] += new
                norm[h] += new_norm
            return carry

        lax.fori_loop(first, first + count, head, 0, unroll=True)

    def start_own(c):
        for j in range(2):
            own(c, j).start()
        if c > last - DIRECT:
            straight(c).start()

    meet(0)
    for c in range(AHEAD):
        start_own(c)
    for load in loads:
        load.wait()
    for c in range(last + 1):
        for j in range(2):
            own(c, j).wait_recv()
            if c <= last - DIRECT:
                forward(c, j).start()
        if c + AHEAD <= last:
            start_own(c + AHEAD)
        if c < 3:
            met_all(c)
            if c < 2:
                meet(c + 1)
        def begin(p, carry, c=c):
            acc[p, pl.ds(*CHUNKS[c]), :] = partial_sum(p, c, (0, 1, 2))
            return carry

        lax.fori_loop(0, 3, begin, 0)
        if c > 0:
            for copy in to_opposite(c - 1):
                copy.wait_recv()

            def finish(p, carry, c=c):
                keep(p, c - 1, acc[p, pl.ds(*CHUNKS[c - 1]), :] + partial_sum(p, c - 1, (3,)))
                return carry

            lax.fori_loop(0, 3, finish, 0)
            add_update(c - 1)

    for copy in to_opposite(last):
        copy.wait_recv()
    mine = core * 8 + chip

    def first_step(i, column):
        return pltpu.make_async_remote_copy(
            src_ref=send1.at[i], dst_ref=got1.at[col], send_sem=s_send.at[0], recv_sem=s_recv.at[0],
            device_id={"ctx": row * ROWDEV + column}, device_id_type=MESH,
        )

    rows = pl.ds(*CHUNKS[last])
    for half in range(2):
        columns = pl.ds(half * 256, 256)
        for p in (1, 2):
            total = acc[p, rows, columns] + dot(tok[3, rows, :], weights[p, sources[3], :, columns])
            total = total.astype(BF16)
            for h in range(2):
                qkv[p, 2 * half + h, rows, :] = total[:, h * HD : (h + 1) * HD]
        add_update(last, 2 * half, 2)
        for h in (2 * half, 2 * half + 1):
            send1[4 * h : 4 * h + 4] = update[h].reshape(4, SLICE, HD).astype(BF16)
        for d in CHIPS_FAR_FIRST:
            to = lax.rem(chip + d, 8)
            first_step(half * 8 + to, to * 2 + half).start()

        @pl.when(core != half)
        def _(half=half):
            first_step(half * 8 + chip, chip * 2 + half).start()

    got1[col] = send1[mine]

    tile_row = lax.broadcasted_iota(jnp.int32, (TILE, HD), 0)
    tile = jnp.zeros((TILE, HD), F32)
    for h in range(HEADS):
        high = norm[h].astype(BF16).astype(F32)
        tile = jnp.where(tile_row == h, high, tile)
        tile = jnp.where(tile_row == HEADS + h, norm[h] - high, tile)
    tile1[...] = tile.astype(BF16)
    for d in FAR_FIRST:
        pltpu.make_async_remote_copy(
            src_ref=tile1, dst_ref=tiles1.at[col], send_sem=s_send.at[3], recv_sem=s_recv.at[3],
            device_id=in_row(d), device_id_type=MESH,
        ).start()
    tiles1[col] = tile1[...]

    def all_of(step, src, dst, count):
        return pltpu.make_async_remote_copy(
            src_ref=src.at[pl.ds(0, count)], dst_ref=dst.at[pl.ds(0, count)],
            send_sem=s_send.at[step], recv_sem=s_recv.at[step],
            device_id=right, device_id_type=MESH,
        )

    def attend(h, carry):
        q, k, v = qkv.at[0, h], qkv.at[1, h], qkv.at[2, h]
        mapped_q[h] = phi(q[...].astype(F32)).astype(BF16)
        share = jax.nn.sigmoid(jnp.full((8, HD), gate_ref[h], F32))[0:1, :]
        for i in range(4):
            mine, seen = pl.ds(i * 128, 128), (i + 1) * 128
            scores = lax.dot_general(
                q[mine, :], k[0:seen, :], (((1,), (1,)), ((), ())), preferred_element_type=F32
            ) * (1.0 / math.sqrt(HD))
            at = lax.broadcasted_iota(jnp.int32, (128, seen), 0) + i * 128
            of = lax.broadcasted_iota(jnp.int32, (128, seen), 1)
            scores = jnp.where(of <= at, scores, -jnp.inf)
            w = jnp.exp(scores - jnp.max(scores, axis=-1, keepdims=True))
            probs = (w / jnp.sum(w, axis=-1, keepdims=True)).astype(BF16)
            local[h, mine, :] = (1.0 - share) * dot(probs, v[0:seen, :])
        return carry

    keep(0, last, acc[0, rows, :] + partial_sum(0, last, (3,)))
    lax.fori_loop(0, 2, attend, 0)
    all_of(0, got1, got1, ROWDEV - 1).wait_recv()

    def second_step(src, dst, step):
        for to in range(1, YS):

            @pl.when(row < to)
            def _(to=to):
                pltpu.make_async_remote_copy(
                    src_ref=src, dst_ref=dst.at[row],
                    send_sem=s_send.at[step], recv_sem=s_recv.at[step],
                    device_id={"ctx": to * ROWDEV + col}, device_id_type=MESH,
                ).start()

    def earlier_rows(dst, step, into):
        into[...] = jnp.zeros_like(into)
        for n in range(1, YS):

            @pl.when(row == n)
            def _(n=n):
                all_of(step, dst, dst, n).wait_recv()
                into[...] = sum(dst[r].astype(F32) for r in range(n))

    total = got1[0].astype(F32)
    for s in range(1, ROWDEV):
        total = total + got1[s].astype(F32)
    send2[...] = total.astype(BF16)
    second_step(send2, got2, 1)
    all_of(3, tiles1, tiles1, ROWDEV - 1).wait_recv()
    total_norm = jnp.zeros((TILE, HD), F32)
    row_norm = jnp.zeros((TILE, HD), F32)
    for s in range(ROWDEV):
        held = tiles1[s].astype(F32)
        total_norm = total_norm + jnp.where(s < col, held, 0.0)
        row_norm = row_norm + held
    tile2[...] = row_norm.astype(BF16)
    second_step(tile2, tiles2, 4)
    running = jnp.zeros((SLICE, HD), F32)
    for s in range(ROWDEV):
        prefix[s] = running
        running = running + got1[s].astype(F32)

    earlier_rows(got2, 1, offset2)
    offset = offset2[...]
    for to in TARGETS:
        send3[to] = (prefix[to] + offset).astype(BF16)

        @pl.when(col != to)
        def _(to=to):
            pltpu.make_async_remote_copy(
                src_ref=send3.at[to], dst_ref=memory.at[mine],
                send_sem=s_send.at[2], recv_sem=s_recv.at[2],
                device_id={"ctx": row * ROWDEV + to}, device_id_type=MESH,
            ).start()

    memory[mine] = (prefix[col] + offset).astype(BF16)
    lax.fori_loop(2, 4, attend, 0)

    earlier_rows(tiles2, 4, offset_tile)
    total_norm = total_norm + offset_tile[...]
    for h in range(HEADS):
        normalizer = total_norm[h : h + 1, :] + total_norm[HEADS + h : HEADS + h + 1, :]
        share = jax.nn.sigmoid(jnp.full((8, HD), gate_ref[h], F32))[0:1, :]
        below = jnp.sum(mapped_q[h].astype(F32) * normalizer, axis=-1, keepdims=True)
        scale[h] = share / jnp.maximum(below, 1.0)
    all_of(2, memory, memory, ROWDEV - 1).wait_recv()

    for h in range(HEADS):
        held = memory[4 * h : 4 * h + 4].reshape(HD, HD)
        out_ref[:, h * HD : (h + 1) * HD] = (
            scale[h] * dot(mapped_q[h], held) + local[h]
        ).astype(BF16)

    for c in range(last + 1):
        for j in range(2):
            own(c, j).wait_send()
        for copy in to_opposite(c):
            copy.wait_send()
    all_of(0, got1, got1, ROWDEV - 1).wait_send()
    all_of(2, memory, memory, ROWDEV - 1).wait_send()
    all_of(3, tiles1, tiles1, ROWDEV - 1).wait_send()
    for n in range(YS - 1):

        @pl.when(row == n)
        def _(n=n):
            all_of(1, got2, got2, YS - 1 - n).wait_send()
            all_of(4, tiles2, tiles2, YS - 1 - n).wait_send()


def per_device(tokens, w_query, w_key, w_value, gate_logit):
    weights = tuple(w.reshape(4, DEPTH, WIDTH) for w in (w_query, w_key, w_value))
    anywhere = pl.BlockSpec(memory_space=pl.ANY)
    steps = len(CHUNKS)
    return pl.pallas_call(
        kernel,
        out_shape=jax.ShapeDtypeStruct((TOK, WIDTH), BF16),
        in_specs=[anywhere] * 5,
        out_specs=pl.BlockSpec(memory_space=pltpu.VMEM),
        scratch_shapes=[
            pltpu.VMEM((4, TOK, DEPTH), BF16),
            pltpu.VMEM((3, 4, DEPTH, WIDTH), BF16),
            pltpu.SMEM((HEADS,), F32),
            pltpu.VMEM((3, HEADS, TOK, HD), BF16),
            pltpu.VMEM((3, TOK, WIDTH), F32),
            pltpu.VMEM((HEADS, HD, HD), F32),
            pltpu.VMEM((HEADS, TILE, HD), F32),
            pltpu.VMEM((HEADS, TOK, HD), BF16),
            pltpu.VMEM((HEADS, TOK, HD), F32),
            pltpu.VMEM((HEADS, TOK, HD), F32),
            pltpu.VMEM((ROWDEV, SLICE, HD), BF16),
            pltpu.VMEM((ROWDEV, SLICE, HD), BF16),
            pltpu.VMEM((TILE, HD), BF16),
            pltpu.VMEM((ROWDEV, TILE, HD), BF16),
            pltpu.VMEM((SLICE, HD), BF16),
            pltpu.VMEM((YS, SLICE, HD), BF16),
            pltpu.VMEM((TILE, HD), BF16),
            pltpu.VMEM((YS, TILE, HD), BF16),
            pltpu.VMEM((ROWDEV, SLICE, HD), F32),
            pltpu.VMEM((SLICE, HD), F32),
            pltpu.VMEM((TILE, HD), F32),
            pltpu.VMEM((ROWDEV, SLICE, HD), BF16),
            pltpu.VMEM((ROWDEV, SLICE, HD), BF16),
            pltpu.SemaphoreType.DMA((5,)),
            pltpu.SemaphoreType.DMA((4, steps)),
            pltpu.SemaphoreType.DMA((4, steps)),
            pltpu.SemaphoreType.DMA((5,)),
            pltpu.SemaphoreType.DMA((5,)),
            pltpu.SemaphoreType.REGULAR((3,)),
        ],
        compiler_params=pltpu.CompilerParams(
            collective_id=0, has_side_effects=True, vmem_limit_bytes=63 << 20
        ),
        cost_estimate=pl.CostEstimate(
            flops=7_400_000_000, bytes_accessed=15_000_000, transcendentals=2_000_000
        ),
    )(tokens, *weights, gate_logit)


def solution(mesh):
    return jax.shard_map(
        per_device,
        mesh=mesh,
        in_specs=(P("ctx", "head"), P(None, "head"), P(None, "head"), P(None, "head"), P("head")),
        out_specs=P("ctx", "head"),
        check_vma=False,
    )
```

```python
import functools
import math

import jax
import jax.numpy as jnp
from jax import lax
from jax.experimental import pallas as pl
from jax.experimental.pallas import tpu as pltpu
from jax.sharding import PartitionSpec as P

MESH = pl.DeviceIdType.MESH
F32, BF16 = jnp.float32, jnp.bfloat16
HD = 128
TOK = 512
WIDTH = 512
DEPTH = 1024
HEADS = 4
ROWDEV = 16
YS = 4
SLICE = 32
TILE = 16
SIZES = (128, 160, 128, 96)
CHUNKS = tuple((sum(SIZES[:i]), n) for i, n in enumerate(SIZES))
AHEAD = 2
DIRECT = 0
FAR_FIRST = (8, 7, 9, 6, 10, 5, 11, 4, 12, 3, 13, 2, 14, 1, 15)
TARGETS = (0, 1, 2, 3, 4, 5, 6, 7, 14, 15, 8, 9, 12, 13, 10, 11)
CHIPS_FAR_FIRST = (4, 3, 5, 2, 6, 1, 7)


def phi(u):
    return jnp.where(u > 0, u + 1.0, jnp.exp(jnp.minimum(u, 0.0)))


def dot(a, b):
    return jnp.dot(a, b, preferred_element_type=F32)


def kernel(
    tok_hbm, wq_hbm, wk_hbm, wv_hbm, gate_hbm, out_ref,
    tok, weights, gate_ref, qkv, acc, update, norm, mapped_q, local, scale,
    send1, got1, tile1, tiles1, send2, got2, tile2, tiles2, prefix, offset2, offset_tile, send3, memory,
    load_sem, x_send, x_recv, s_send, s_recv, met,
):
    me = lax.axis_index("ctx")
    x = lax.axis_index("head")
    col, row = lax.rem(me, ROWDEV), me // ROWDEV
    chip, core = col // 2, lax.rem(col, 2)
    right, left = {"head": lax.rem(x + 1, 4)}, {"head": lax.rem(x + 3, 4)}
    sides = (right, left)

    def in_row(d):
        return {"ctx": row * ROWDEV + lax.rem(col + d, ROWDEV)}

    def in_column(d):
        return {"ctx": lax.rem(row + d, YS) * ROWDEV + col}

    loads = [
        pltpu.make_async_copy(tok_hbm, tok.at[0], load_sem.at[0]),
        pltpu.make_async_copy(gate_hbm, gate_ref, load_sem.at[4]),
    ]
    for p, w in enumerate((wq_hbm, wk_hbm, wv_hbm)):
        loads.append(pltpu.make_async_copy(w, weights.at[p], load_sem.at[1 + p]))
    for load in loads:
        load.start()

    barrier = pltpu.get_barrier_semaphore()
    near = [in_row(2), in_row(14), in_column(1), in_column(3)]
    other = {"ctx": me + 1 - 2 * lax.rem(me, 2)}
    for target in near + [other, right, left]:
        pl.semaphore_signal(barrier, inc=1, device_id=target, device_id_type=MESH)
    pl.semaphore_wait(barrier, len(near) + 3)

    def meet(step):
        for target in (near, [in_row(4), in_row(12)], [in_row(8)])[step]:
            pl.semaphore_signal(met.at[step], inc=1, device_id=target, device_id_type=MESH)

    def met_all(step):
        pl.semaphore_wait(met.at[step], (4, 2, 1)[step])

    def own(c, j):
        rows = pl.ds(*CHUNKS[c])
        return pltpu.make_async_remote_copy(
            src_ref=tok_hbm.at[rows], dst_ref=tok.at[1 + j, rows],
            send_sem=x_send.at[j, c], recv_sem=x_recv.at[j, c],
            device_id=sides[j], device_id_type=MESH,
        )

    last = len(CHUNKS) - 1

    def forward(c, j):
        first, count = CHUNKS[c]
        rows = pl.ds(first + j * (count // 2), count // 2)
        return pltpu.make_async_remote_copy(
            src_ref=tok.at[1 + j, rows], dst_ref=tok.at[3, rows],
            send_sem=x_send.at[2 + j, c], recv_sem=x_recv.at[2 + j, c],
            device_id=sides[j], device_id_type=MESH,
        )

    def straight(c):
        rows = pl.ds(*CHUNKS[c])
        return pltpu.make_async_remote_copy(
            src_ref=tok_hbm.at[rows], dst_ref=tok.at[3, rows],
            send_sem=x_send.at[2, c], recv_sem=x_recv.at[2, c],
            device_id={"head": lax.rem(x + 2, 4)}, device_id_type=MESH,
        )

    def to_opposite(c):
        return [straight(c)] if c > last - DIRECT else [forward(c, 0), forward(c, 1)]

    sources = (x, lax.rem(x + 3, 4), lax.rem(x + 1, 4), lax.rem(x + 2, 4))

    def partial_sum(p, c, which):
        rows = pl.ds(*CHUNKS[c])
        return sum(dot(tok[s, rows, :], weights[p, sources[s]]) for s in which)

    def keep(p, c, total):
        total = total.astype(BF16)
        for h in range(HEADS):
            qkv[p, h, pl.ds(*CHUNKS[c]), :] = total[:, h * HD : (h + 1) * HD]

    def add_update(c, first=0, count=HEADS):
        rows = pl.ds(*CHUNKS[c])

        def head(h, carry):
            mapped = phi(qkv[1, h, rows, :].astype(F32)).astype(BF16)
            new = lax.dot_general(
                mapped, qkv[2, h, rows, :], (((0,), (0,)), ((), ())), preferred_element_type=F32
            )
            new_norm = dot(jnp.ones((TILE, CHUNKS[c][1]), BF16), mapped)
            if c == 0:
                update[h] = new
                norm[h] = new_norm
            else:
                update[h] += new
                norm[h] += new_norm
            return carry

        lax.fori_loop(first, first + count, head, 0, unroll=True)

    def start_own(c):
        for j in range(2):
            own(c, j).start()
        if c > last - DIRECT:
            straight(c).start()

    meet(0)
    for c in range(AHEAD):
        start_own(c)
    for load in loads:
        load.wait()
    for c in range(last + 1):
        for j in range(2):
            own(c, j).wait_recv()
            if c <= last - DIRECT:
                forward(c, j).start()
        if c + AHEAD <= last:
            start_own(c + AHEAD)
        if c < 3:
            met_all(c)
            if c < 2:
                meet(c + 1)
        def begin(p, carry, c=c):
            acc[p, pl.ds(*CHUNKS[c]), :] = partial_sum(p, c, (0, 1, 2))
            return carry

        lax.fori_loop(0, 3, begin, 0)
        if c > 0:
            for copy in to_opposite(c - 1):
                copy.wait_recv()

            def finish(p, carry, c=c):
                keep(p, c - 1, acc[p, pl.ds(*CHUNKS[c - 1]), :] + partial_sum(p, c - 1, (3,)))
                return carry

            lax.fori_loop(0, 3, finish, 0)
            add_update(c - 1)

    for copy in to_opposite(last):
        copy.wait_recv()
    mine = core * 8 + chip

    def first_step(i, column):
        return pltpu.make_async_remote_copy(
            src_ref=send1.at[i], dst_ref=got1.at[col], send_sem=s_send.at[0], recv_sem=s_recv.at[0],
            device_id={"ctx": row * ROWDEV + column}, device_id_type=MESH,
        )

    rows = pl.ds(*CHUNKS[last])
    for half in range(2):
        columns = pl.ds(half * 256, 256)
        for p in (1, 2):
            total = acc[p, rows, columns] + dot(tok[3, rows, :], weights[p, sources[3], :, columns])
            total = total.astype(BF16)
            for h in range(2):
                qkv[p, 2 * half + h, rows, :] = total[:, h * HD : (h + 1) * HD]
        add_update(last, 2 * half, 2)
        for h in (2 * half, 2 * half + 1):
            send1[4 * h : 4 * h + 4] = update[h].reshape(4, SLICE, HD).astype(BF16)
        for d in CHIPS_FAR_FIRST:
            to = lax.rem(chip + d, 8)
            first_step(half * 8 + to, to * 2 + half).start()

        @pl.when(core != half)
        def _(half=half):
            first_step(half * 8 + chip, chip * 2 + half).start()

    got1[col] = send1[mine]

    tile_row = lax.broadcasted_iota(jnp.int32, (TILE, HD), 0)
    tile = jnp.zeros((TILE, HD), F32)
    for h in range(HEADS):
        high = norm[h].astype(BF16).astype(F32)
        tile = jnp.where(tile_row == h, high, tile)
        tile = jnp.where(tile_row == HEADS + h, norm[h] - high, tile)
    tile1[...] = tile.astype(BF16)
    for d in FAR_FIRST:
        pltpu.make_async_remote_copy(
            src_ref=tile1, dst_ref=tiles1.at[col], send_sem=s_send.at[3], recv_sem=s_recv.at[3],
            device_id=in_row(d), device_id_type=MESH,
        ).start()
    tiles1[col] = tile1[...]

    def all_of(step, src, dst, count):
        return pltpu.make_async_remote_copy(
            src_ref=src.at[pl.ds(0, count)], dst_ref=dst.at[pl.ds(0, count)],
            send_sem=s_send.at[step], recv_sem=s_recv.at[step],
            device_id=right, device_id_type=MESH,
        )

    def attend(h, carry):
        q, k, v = qkv.at[0, h], qkv.at[1, h], qkv.at[2, h]
        mapped_q[h] = phi(q[...].astype(F32)).astype(BF16)
        share = jax.nn.sigmoid(jnp.full((8, HD), gate_ref[h], F32))[0:1, :]
        for i in range(4):
            mine, seen = pl.ds(i * 128, 128), (i + 1) * 128
            scores = lax.dot_general(
                q[mine, :], k[0:seen, :], (((1,), (1,)), ((), ())), preferred_element_type=F32
            ) * (1.0 / math.sqrt(HD))
            at = lax.broadcasted_iota(jnp.int32, (128, seen), 0) + i * 128
            of = lax.broadcasted_iota(jnp.int32, (128, seen), 1)
            scores = jnp.where(of <= at, scores, -jnp.inf)
            w = jnp.exp(scores - jnp.max(scores, axis=-1, keepdims=True))
            probs = (w / jnp.sum(w, axis=-1, keepdims=True)).astype(BF16)
            local[h, mine, :] = (1.0 - share) * dot(probs, v[0:seen, :])
        return carry

    keep(0, last, acc[0, rows, :] + partial_sum(0, last, (3,)))
    lax.fori_loop(0, 2, attend, 0)
    all_of(0, got1, got1, ROWDEV - 1).wait_recv()

    def second_step(src, dst, step):
        for to in range(1, YS):

            @pl.when(row < to)
            def _(to=to):
                pltpu.make_async_remote_copy(
                    src_ref=src, dst_ref=dst.at[row],
                    send_sem=s_send.at[step], recv_sem=s_recv.at[step],
                    device_id={"ctx": to * ROWDEV + col}, device_id_type=MESH,
                ).start()

    def earlier_rows(dst, step, into):
        into[...] = jnp.zeros_like(into)
        for n in range(1, YS):

            @pl.when(row == n)
            def _(n=n):
                all_of(step, dst, dst, n).wait_recv()
                into[...] = sum(dst[r].astype(F32) for r in range(n))

    total = got1[0].astype(F32)
    for s in range(1, ROWDEV):
        total = total + got1[s].astype(F32)
    send2[...] = total.astype(BF16)
    second_step(send2, got2, 1)
    running = jnp.zeros((SLICE, HD), F32)
    for s in range(ROWDEV):
        prefix[s] = running
        running = running + got1[s].astype(F32)

    earlier_rows(got2, 1, offset2)
    offset = offset2[...]
    for to in TARGETS:
        send3[to] = (prefix[to] + offset).astype(BF16)

        @pl.when(col != to)
        def _(to=to):
            pltpu.make_async_remote_copy(
                src_ref=send3.at[to], dst_ref=memory.at[mine],
                send_sem=s_send.at[2], recv_sem=s_recv.at[2],
                device_id={"ctx": row * ROWDEV + to}, device_id_type=MESH,
            ).start()

    memory[mine] = (prefix[col] + offset).astype(BF16)
    all_of(3, tiles1, tiles1, ROWDEV - 1).wait_recv()
    total_norm = jnp.zeros((TILE, HD), F32)
    row_norm = jnp.zeros((TILE, HD), F32)
    for s in range(ROWDEV):
        held = tiles1[s].astype(F32)
        total_norm = total_norm + jnp.where(s < col, held, 0.0)
        row_norm = row_norm + held
    tile2[...] = row_norm.astype(BF16)
    second_step(tile2, tiles2, 4)
    lax.fori_loop(2, 4, attend, 0)

    earlier_rows(tiles2, 4, offset_tile)
    total_norm = total_norm + offset_tile[...]
    for h in range(HEADS):
        normalizer = total_norm[h : h + 1, :] + total_norm[HEADS + h : HEADS + h + 1, :]
        share = jax.nn.sigmoid(jnp.full((8, HD), gate_ref[h], F32))[0:1, :]
        below = jnp.sum(mapped_q[h].astype(F32) * normalizer, axis=-1, keepdims=True)
        scale[h] = share / jnp.maximum(below, 1.0)
    all_of(2, memory, memory, ROWDEV - 1).wait_recv()

    for h in range(HEADS):
        held = memory[4 * h : 4 * h + 4].reshape(HD, HD)
        out_ref[:, h * HD : (h + 1) * HD] = (
            scale[h] * dot(mapped_q[h], held) + local[h]
        ).astype(BF16)

    for c in range(last + 1):
        for j in range(2):
            own(c, j).wait_send()
        for copy in to_opposite(c):
            copy.wait_send()
    all_of(0, got1, got1, ROWDEV - 1).wait_send()
    all_of(2, memory, memory, ROWDEV - 1).wait_send()
    all_of(3, tiles1, tiles1, ROWDEV - 1).wait_send()
    for n in range(YS - 1):

        @pl.when(row == n)
        def _(n=n):
            all_of(1, got2, got2, YS - 1 - n).wait_send()
            all_of(4, tiles2, tiles2, YS - 1 - n).wait_send()


def per_device(tokens, w_query, w_key, w_value, gate_logit):
    weights = tuple(w.reshape(4, DEPTH, WIDTH) for w in (w_query, w_key, w_value))
    anywhere = pl.BlockSpec(memory_space=pl.ANY)
    steps = len(CHUNKS)
    return pl.pallas_call(
        kernel,
        out_shape=jax.ShapeDtypeStruct((TOK, WIDTH), BF16),
        in_specs=[anywhere] * 5,
        out_specs=pl.BlockSpec(memory_space=pltpu.VMEM),
        scratch_shapes=[
            pltpu.VMEM((4, TOK, DEPTH), BF16),
            pltpu.VMEM((3, 4, DEPTH, WIDTH), BF16),
            pltpu.SMEM((HEADS,), F32),
            pltpu.VMEM((3, HEADS, TOK, HD), BF16),
            pltpu.VMEM((3, TOK, WIDTH), F32),
            pltpu.VMEM((HEADS, HD, HD), F32),
            pltpu.VMEM((HEADS, TILE, HD), F32),
            pltpu.VMEM((HEADS, TOK, HD), BF16),
            pltpu.VMEM((HEADS, TOK, HD), F32),
            pltpu.VMEM((HEADS, TOK, HD), F32),
            pltpu.VMEM((ROWDEV, SLICE, HD), BF16),
            pltpu.VMEM((ROWDEV, SLICE, HD), BF16),
            pltpu.VMEM((TILE, HD), BF16),
            pltpu.VMEM((ROWDEV, TILE, HD), BF16),
            pltpu.VMEM((SLICE, HD), BF16),
            pltpu.VMEM((YS, SLICE, HD), BF16),
            pltpu.VMEM((TILE, HD), BF16),
            pltpu.VMEM((YS, TILE, HD), BF16),
            pltpu.VMEM((ROWDEV, SLICE, HD), F32),
            pltpu.VMEM((SLICE, HD), F32),
            pltpu.VMEM((TILE, HD), F32),
            pltpu.VMEM((ROWDEV, SLICE, HD), BF16),
            pltpu.VMEM((ROWDEV, SLICE, HD), BF16),
            pltpu.SemaphoreType.DMA((5,)),
            pltpu.SemaphoreType.DMA((4, steps)),
            pltpu.SemaphoreType.DMA((4, steps)),
            pltpu.SemaphoreType.DMA((5,)),
            pltpu.SemaphoreType.DMA((5,)),
            pltpu.SemaphoreType.REGULAR((3,)),
        ],
        compiler_params=pltpu.CompilerParams(
            collective_id=0, has_side_effects=True, vmem_limit_bytes=63 << 20
        ),
        cost_estimate=pl.CostEstimate(
            flops=7_400_000_000, bytes_accessed=15_000_000, transcendentals=2_000_000
        ),
    )(tokens, *weights, gate_logit)


def solution(mesh):
    return jax.shard_map(
        per_device,
        mesh=mesh,
        in_specs=(P("ctx", "head"), P(None, "head"), P(None, "head"), P(None, "head"), P("head")),
        out_specs=P("ctx", "head"),
        check_vma=False,
    )
```

```python
import functools
import math

import jax
import jax.numpy as jnp
from jax import lax
from jax.experimental import pallas as pl
from jax.experimental.pallas import tpu as pltpu
from jax.sharding import PartitionSpec as P

MESH = pl.DeviceIdType.MESH
F32, BF16 = jnp.float32, jnp.bfloat16
HD = 128
TOK = 512
WIDTH = 512
DEPTH = 1024
HEADS = 4
ROWDEV = 16
YS = 4
SLICE = 32
TILE = 16
SIZES = (128, 160, 128, 96)
CHUNKS = tuple((sum(SIZES[:i]), n) for i, n in enumerate(SIZES))
AHEAD = 2
DIRECT = 0
FAR_FIRST = (8, 7, 9, 6, 10, 5, 11, 4, 12, 3, 13, 2, 14, 1, 15)
TARGETS = (0, 1, 2, 3, 4, 5, 6, 7, 14, 15, 8, 9, 12, 13, 10, 11)
CHIPS_FAR_FIRST = (4, 3, 5, 2, 6, 1, 7)


def phi(u):
    return jnp.where(u > 0, u + 1.0, jnp.exp(jnp.minimum(u, 0.0)))


def dot(a, b):
    return jnp.dot(a, b, preferred_element_type=F32)


def kernel(
    tok_hbm, wq_hbm, wk_hbm, wv_hbm, gate_hbm, out_ref,
    tok, weights, gate_ref, qkv, acc, update, norm, mapped_q, local, scale,
    send1, got1, tile1, tiles1, send2, got2, tile2, tiles2, prefix, offset2, offset_tile, send3, memory,
    load_sem, x_send, x_recv, s_send, s_recv, met,
):
    me = lax.axis_index("ctx")
    x = lax.axis_index("head")
    col, row = lax.rem(me, ROWDEV), me // ROWDEV
    chip, core = col // 2, lax.rem(col, 2)
    right, left = {"head": lax.rem(x + 1, 4)}, {"head": lax.rem(x + 3, 4)}
    sides = (right, left)

    def in_row(d):
        return {"ctx": row * ROWDEV + lax.rem(col + d, ROWDEV)}

    def in_column(d):
        return {"ctx": lax.rem(row + d, YS) * ROWDEV + col}

    loads = [
        pltpu.make_async_copy(tok_hbm, tok.at[0], load_sem.at[0]),
        pltpu.make_async_copy(gate_hbm, gate_ref, load_sem.at[4]),
    ]
    for p, w in enumerate((wq_hbm, wk_hbm, wv_hbm)):
        loads.append(pltpu.make_async_copy(w, weights.at[p], load_sem.at[1 + p]))
    for load in loads:
        load.start()

    barrier = pltpu.get_barrier_semaphore()
    near = [in_row(2), in_row(14), in_column(1), in_column(3)]
    other = {"ctx": me + 1 - 2 * lax.rem(me, 2)}
    for target in near + [other, right, left]:
        pl.semaphore_signal(barrier, inc=1, device_id=target, device_id_type=MESH)
    pl.semaphore_wait(barrier, len(near) + 3)

    def meet(step):
        for target in (near, [in_row(4), in_row(12)], [in_row(8)])[step]:
            pl.semaphore_signal(met.at[step], inc=1, device_id=target, device_id_type=MESH)

    def met_all(step):
        pl.semaphore_wait(met.at[step], (4, 2, 1)[step])

    def own(c, j):
        rows = pl.ds(*CHUNKS[c])
        return pltpu.make_async_remote_copy(
            src_ref=tok_hbm.at[rows], dst_ref=tok.at[1 + j, rows],
            send_sem=x_send.at[j, c], recv_sem=x_recv.at[j, c],
            device_id=sides[j], device_id_type=MESH,
        )

    last = len(CHUNKS) - 1

    def forward(c, j):
        first, count = CHUNKS[c]
        rows = pl.ds(first + j * (count // 2), count // 2)
        return pltpu.make_async_remote_copy(
            src_ref=tok.at[1 + j, rows], dst_ref=tok.at[3, rows],
            send_sem=x_send.at[2 + j, c], recv_sem=x_recv.at[2 + j, c],
            device_id=sides[j], device_id_type=MESH,
        )

    def straight(c):
        rows = pl.ds(*CHUNKS[c])
        return pltpu.make_async_remote_copy(
            src_ref=tok_hbm.at[rows], dst_ref=tok.at[3, rows],
            send_sem=x_send.at[2, c], recv_sem=x_recv.at[2, c],
            device_id={"head": lax.rem(x + 2, 4)}, device_id_type=MESH,
        )

    def to_opposite(c):
        return [straight(c)] if c > last - DIRECT else [forward(c, 0), forward(c, 1)]

    sources = (x, lax.rem(x + 3, 4), lax.rem(x + 1, 4), lax.rem(x + 2, 4))

    def partial_sum(p, c, which):
        rows = pl.ds(*CHUNKS[c])
        return sum(dot(tok[s, rows, :], weights[p, sources[s]]) for s in which)

    def keep(p, c, total):
        total = total.astype(BF16)
        for h in range(HEADS):
            qkv[p, h, pl.ds(*CHUNKS[c]), :] = total[:, h * HD : (h + 1) * HD]

    def add_update(c, first=0, count=HEADS):
        rows = pl.ds(*CHUNKS[c])

        def head(h, carry):
            mapped = phi(qkv[1, h, rows, :].astype(F32)).astype(BF16)
            new = lax.dot_general(
                mapped, qkv[2, h, rows, :], (((0,), (0,)), ((), ())), preferred_element_type=F32
            )
            new_norm = dot(jnp.ones((TILE, CHUNKS[c][1]), BF16), mapped)
            if c == 0:
                update[h] = new
                norm[h] = new_norm
            else:
                update[h] += new
                norm[h] += new_norm
            return carry

        lax.fori_loop(first, first + count, head, 0, unroll=True)

    def start_own(c):
        for j in range(2):
            own(c, j).start()
        if c > last - DIRECT:
            straight(c).start()

    meet(0)
    for c in range(AHEAD):
        start_own(c)
    for load in loads:
        load.wait()
    for c in range(last + 1):
        for j in range(2):
            own(c, j).wait_recv()
            if c <= last - DIRECT:
                forward(c, j).start()
        if c + AHEAD <= last:
            start_own(c + AHEAD)
        if c < 3:
            met_all(c)
            if c < 2:
                meet(c + 1)
        def begin(p, carry, c=c):
            acc[p, pl.ds(*CHUNKS[c]), :] = partial_sum(p, c, (0, 1, 2))
            return carry

        lax.fori_loop(0, 3, begin, 0)
        if c > 0:
            for copy in to_opposite(c - 1):
                copy.wait_recv()

            def finish(p, carry, c=c):
                keep(p, c - 1, acc[p, pl.ds(*CHUNKS[c - 1]), :] + partial_sum(p, c - 1, (3,)))
                return carry

            lax.fori_loop(0, 3, finish, 0)
            add_update(c - 1)

    for copy in to_opposite(last):
        copy.wait_recv()
    mine = core * 8 + chip

    def first_step(i, column):
        return pltpu.make_async_remote_copy(
            src_ref=send1.at[i], dst_ref=got1.at[col], send_sem=s_send.at[0], recv_sem=s_recv.at[0],
            device_id={"ctx": row * ROWDEV + column}, device_id_type=MESH,
        )

    rows = pl.ds(*CHUNKS[last])
    for half in range(2):
        columns = pl.ds(half * 256, 256)
        for p in (1, 2):
            total = acc[p, rows, columns] + dot(tok[3, rows, :], weights[p, sources[3], :, columns])
            total = total.astype(BF16)
            for h in range(2):
                qkv[p, 2 * half + h, rows, :] = total[:, h * HD : (h + 1) * HD]
        add_update(last, 2 * half, 2)
        for h in (2 * half, 2 * half + 1):
            send1[4 * h : 4 * h + 4] = update[h].reshape(4, SLICE, HD).astype(BF16)
        for d in CHIPS_FAR_FIRST:
            to = lax.rem(chip + d, 8)
            first_step(half * 8 + to, to * 2 + half).start()

        @pl.when(core != half)
        def _(half=half):
            first_step(half * 8 + chip, chip * 2 + half).start()

    got1[col] = send1[mine]

    tile_row = lax.broadcasted_iota(jnp.int32, (TILE, HD), 0)
    tile = jnp.zeros((TILE, HD), F32)
    for h in range(HEADS):
        high = norm[h].astype(BF16).astype(F32)
        tile = jnp.where(tile_row == h, high, tile)
        tile = jnp.where(tile_row == HEADS + h, norm[h] - high, tile)
    tile1[...] = tile.astype(BF16)
    for d in FAR_FIRST:
        pltpu.make_async_remote_copy(
            src_ref=tile1, dst_ref=tiles1.at[col], send_sem=s_send.at[3], recv_sem=s_recv.at[3],
            device_id=in_row(d), device_id_type=MESH,
        ).start()
    tiles1[col] = tile1[...]

    def all_of(step, src, dst, count):
        return pltpu.make_async_remote_copy(
            src_ref=src.at[pl.ds(0, count)], dst_ref=dst.at[pl.ds(0, count)],
            send_sem=s_send.at[step], recv_sem=s_recv.at[step],
            device_id=right, device_id_type=MESH,
        )

    def attend(h, carry):
        q, k, v = qkv.at[0, h], qkv.at[1, h], qkv.at[2, h]
        mapped_q[h] = phi(q[...].astype(F32)).astype(BF16)
        share = jax.nn.sigmoid(jnp.full((8, HD), gate_ref[h], F32))[0:1, :]
        for i in range(4):
            mine, seen = pl.ds(i * 128, 128), (i + 1) * 128
            scores = lax.dot_general(
                q[mine, :], k[0:seen, :], (((1,), (1,)), ((), ())), preferred_element_type=F32
            ) * (1.0 / math.sqrt(HD))
            at = lax.broadcasted_iota(jnp.int32, (128, seen), 0) + i * 128
            of = lax.broadcasted_iota(jnp.int32, (128, seen), 1)
            scores = jnp.where(of <= at, scores, -jnp.inf)
            w = jnp.exp(scores - jnp.max(scores, axis=-1, keepdims=True))
            probs = (w / jnp.sum(w, axis=-1, keepdims=True)).astype(BF16)
            local[h, mine, :] = (1.0 - share) * dot(probs, v[0:seen, :])
        return carry

    keep(0, last, acc[0, rows, :] + partial_sum(0, last, (3,)))
    lax.fori_loop(0, 2, attend, 0)
    all_of(0, got1, got1, ROWDEV - 1).wait_recv()

    def second_step(src, dst, step):
        for to in range(1, YS):

            @pl.when(row < to)
            def _(to=to):
                pltpu.make_async_remote_copy(
                    src_ref=src, dst_ref=dst.at[row],
                    send_sem=s_send.at[step], recv_sem=s_recv.at[step],
                    device_id={"ctx": to * ROWDEV + col}, device_id_type=MESH,
                ).start()

    def earlier_rows(dst, step, into):
        into[...] = jnp.zeros_like(into)
        for n in range(1, YS):

            @pl.when(row == n)
            def _(n=n):
                all_of(step, dst, dst, n).wait_recv()
                into[...] = sum(dst[r].astype(F32) for r in range(n))

    running = jnp.zeros((SLICE, HD), F32)
    for s in range(ROWDEV):
        prefix[s] = running
        running = running + got1[s].astype(F32)
    send2[...] = running.astype(BF16)
    second_step(send2, got2, 1)

    earlier_rows(got2, 1, offset2)
    offset = offset2[...]
    for to in TARGETS:
        send3[to] = (prefix[to] + offset).astype(BF16)

        @pl.when(col != to)
        def _(to=to):
            pltpu.make_async_remote_copy(
                src_ref=send3.at[to], dst_ref=memory.at[mine],
                send_sem=s_send.at[2], recv_sem=s_recv.at[2],
                device_id={"ctx": row * ROWDEV + to}, device_id_type=MESH,
            ).start()

    memory[mine] = (prefix[col] + offset).astype(BF16)
    all_of(3, tiles1, tiles1, ROWDEV - 1).wait_recv()
    total_norm = jnp.zeros((TILE, HD), F32)
    row_norm = jnp.zeros((TILE, HD), F32)
    for s in range(ROWDEV):
        held = tiles1[s].astype(F32)
        total_norm = total_norm + jnp.where(s < col, held, 0.0)
        row_norm = row_norm + held
    tile2[...] = row_norm.astype(BF16)
    second_step(tile2, tiles2, 4)
    lax.fori_loop(2, 4, attend, 0)

    earlier_rows(tiles2, 4, offset_tile)
    total_norm = total_norm + offset_tile[...]
    for h in range(HEADS):
        normalizer = total_norm[h : h + 1, :] + total_norm[HEADS + h : HEADS + h + 1, :]
        share = jax.nn.sigmoid(jnp.full((8, HD), gate_ref[h], F32))[0:1, :]
        below = jnp.sum(mapped_q[h].astype(F32) * normalizer, axis=-1, keepdims=True)
        scale[h] = share / jnp.maximum(below, 1.0)
    all_of(2, memory, memory, ROWDEV - 1).wait_recv()

    for h in range(HEADS):
        held = memory[4 * h : 4 * h + 4].reshape(HD, HD)
        out_ref[:, h * HD : (h + 1) * HD] = (
            scale[h] * dot(mapped_q[h], held) + local[h]
        ).astype(BF16)

    for c in range(last + 1):
        for j in range(2):
            own(c, j).wait_send()
        for copy in to_opposite(c):
            copy.wait_send()
    all_of(0, got1, got1, ROWDEV - 1).wait_send()
    all_of(2, memory, memory, ROWDEV - 1).wait_send()
    all_of(3, tiles1, tiles1, ROWDEV - 1).wait_send()
    for n in range(YS - 1):

        @pl.when(row == n)
        def _(n=n):
            all_of(1, got2, got2, YS - 1 - n).wait_send()
            all_of(4, tiles2, tiles2, YS - 1 - n).wait_send()


def per_device(tokens, w_query, w_key, w_value, gate_logit):
    weights = tuple(w.reshape(4, DEPTH, WIDTH) for w in (w_query, w_key, w_value))
    anywhere = pl.BlockSpec(memory_space=pl.ANY)
    steps = len(CHUNKS)
    return pl.pallas_call(
        kernel,
        out_shape=jax.ShapeDtypeStruct((TOK, WIDTH), BF16),
        in_specs=[anywhere] * 5,
        out_specs=pl.BlockSpec(memory_space=pltpu.VMEM),
        scratch_shapes=[
            pltpu.VMEM((4, TOK, DEPTH), BF16),
            pltpu.VMEM((3, 4, DEPTH, WIDTH), BF16),
            pltpu.SMEM((HEADS,), F32),
            pltpu.VMEM((3, HEADS, TOK, HD), BF16),
            pltpu.VMEM((3, TOK, WIDTH), F32),
            pltpu.VMEM((HEADS, HD, HD), F32),
            pltpu.VMEM((HEADS, TILE, HD), F32),
            pltpu.VMEM((HEADS, TOK, HD), BF16),
            pltpu.VMEM((HEADS, TOK, HD), F32),
            pltpu.VMEM((HEADS, TOK, HD), F32),
            pltpu.VMEM((ROWDEV, SLICE, HD), BF16),
            pltpu.VMEM((ROWDEV, SLICE, HD), BF16),
            pltpu.VMEM((TILE, HD), BF16),
            pltpu.VMEM((ROWDEV, TILE, HD), BF16),
            pltpu.VMEM((SLICE, HD), BF16),
            pltpu.VMEM((YS, SLICE, HD), BF16),
            pltpu.VMEM((TILE, HD), BF16),
            pltpu.VMEM((YS, TILE, HD), BF16),
            pltpu.VMEM((ROWDEV, SLICE, HD), F32),
            pltpu.VMEM((SLICE, HD), F32),
            pltpu.VMEM((TILE, HD), F32),
            pltpu.VMEM((ROWDEV, SLICE, HD), BF16),
            pltpu.VMEM((ROWDEV, SLICE, HD), BF16),
            pltpu.SemaphoreType.DMA((5,)),
            pltpu.SemaphoreType.DMA((4, steps)),
            pltpu.SemaphoreType.DMA((4, steps)),
            pltpu.SemaphoreType.DMA((5,)),
            pltpu.SemaphoreType.DMA((5,)),
            pltpu.SemaphoreType.REGULAR((3,)),
        ],
        compiler_params=pltpu.CompilerParams(
            collective_id=0, has_side_effects=True, vmem_limit_bytes=63 << 20
        ),
        cost_estimate=pl.CostEstimate(
            flops=7_400_000_000, bytes_accessed=15_000_000, transcendentals=2_000_000
        ),
    )(tokens, *weights, gate_logit)


def solution(mesh):
    return jax.shard_map(
        per_device,
        mesh=mesh,
        in_specs=(P("ctx", "head"), P(None, "head"), P(None, "head"), P(None, "head"), P("head")),
        out_specs=P("ctx", "head"),
        check_vma=False,
    )
```
